128 devices in a mesh: grp: 4 (over y_lo, core), ep: 32 (over x, y_hi, z).
Axes of the slice: x: 4, y: 4 (y_hi: 2, y_lo: 2; y = y_hi * 2 + y_lo), z: 4, core: 2. Of those that a mesh axis runs over, the one named last changes fastest.
Arguments:
- cotangent: bfloat16 [16384, 3584], P(('grp', 'ep')), may hold values from -4 to 4
- routes: int32 [16384, 4], P(('grp', 'ep')), may hold values from 0 to 31, as said below
- gates: float32 [16384, 4], P(('grp', 'ep')), may hold values from 0.05 to 1
- pre_act: bfloat16 [16384, 4, 2048], P(('grp', 'ep')), may hold values from -6 to 6
- down_weight: bfloat16 [32, 1024, 3584], P('ep'), may hold values from -0.1875 to 0.1875
Outputs:
- pre_grad: bfloat16 [16384, 4, 2048], P(('grp', 'ep'))
- weight_grad: bfloat16 [32, 1024, 3584], P('ep', 'grp')
The draws below stay inside these ranges and needn't reach their ends.
Inputs may be any that keep to these rules, and one draw needn't show every extreme that they name: `routes`: each row names 4 different experts. In every block of 128 rows one expert, the same in all blocks, is named exactly 96 times; one other expert, the same in all blocks, exactly 20 times; every remaining expert 1 to 20 times.
All inputs are finite; a program needn't handle non-finite values.
Results may differ from the reference program's by a relative error of at most 0.025.
Values may be sent and summed in bfloat16 or wider, within the bound.
A program may use at most 128 MiB of HBM per device.

```python
import math
import jax
import jax.numpy as jnp
from jax import lax

D = 3584
HID = 1024
TOPK = 4
TOK_DEV = 128
EXPERTS = 32
TOKENS = 16384
HOT_ROWS = 96
CAP = 20
N_GRP = 4
N_EP = 32


def route_block(block_key, hot_expert, full_index):
    order_key, move_key, row_key, roll_key = jax.random.split(block_key, 4)
    cold_count = EXPERTS - 1
    rest_load = TOK_DEV * TOPK - HOT_ROWS - CAP
    base_load = rest_load // (cold_count - 1)
    extra_load = rest_load % (cold_count - 1)
    others = jax.random.permutation(order_key, cold_count - 1).astype(jnp.int32)
    others = others + (others >= full_index).astype(jnp.int32)
    cold_order = jnp.concatenate([jnp.reshape(full_index, (1,)).astype(jnp.int32), others])
    position = jnp.arange(cold_count, dtype=jnp.int32)
    later = position - 1
    paired = (position >= 1) & (later < 2 * ((cold_count - 1) // 2))
    move_sizes = jax.random.randint(move_key, (cold_count,), 0, base_load // 3 + 1, dtype=jnp.int32)
    pair_move = move_sizes[jnp.clip(later // 2, 0, cold_count - 1)]
    direction = jnp.where(later % 2 == 0, 1, -1).astype(jnp.int32)
    cold_load = base_load + (later < extra_load).astype(jnp.int32) + jnp.where(paired, direction * pair_move, 0)
    cold_load = jnp.where(position == 0, CAP, cold_load).astype(jnp.int32)
    expert_of = cold_order + (cold_order >= hot_expert).astype(jnp.int32)
    everyone = jnp.arange(EXPERTS, dtype=jnp.int32)
    all_loads = jnp.sum(jnp.where(expert_of[:, None] == everyone[None, :], cold_load[:, None], 0), axis=0)
    all_loads = (all_loads + jnp.where(everyone == hot_expert, HOT_ROWS, 0)).astype(jnp.int32)
    bounds = jnp.cumsum(all_loads).astype(jnp.int32)
    flat_index = jnp.arange(TOK_DEV * TOPK, dtype=jnp.int32)
    listing = jnp.sum((bounds[None, :] <= flat_index[:, None]).astype(jnp.int32), axis=1)
    routing = listing.reshape(TOPK, TOK_DEV).T
    row_order = jax.random.permutation(row_key, TOK_DEV)
    routing = routing[row_order]
    slot_shift = jax.random.randint(roll_key, (TOK_DEV, 1), 0, TOPK, dtype=jnp.int32)
    column = (jnp.arange(TOPK, dtype=jnp.int32)[None, :] + slot_shift) % TOPK
    return jnp.take_along_axis(routing, column, axis=1)


def draw_routes(key, part):
    key = jax.random.fold_in(key, 7)
    hot_key, full_key, block_key = jax.random.split(key, 3)
    hot_expert = jax.random.randint(hot_key, (), 0, EXPERTS, dtype=jnp.int32)
    full_index = jax.random.randint(full_key, (), 0, EXPERTS - 1, dtype=jnp.int32)
    block_keys = jax.random.split(block_key, TOKENS // TOK_DEV)
    blocks = jax.vmap(route_block, in_axes=(0, None, None))(block_keys, hot_expert, full_index)
    return blocks.reshape(TOKENS, TOPK).astype(jnp.int32)


def steps_of(stream_key, extent, cuts, smallest, largest):
    factor_of, own = 1.0, jax.random.fold_in(stream_key, 6)
    for dim, parts in cuts:
        draws = jnp.exp(jax.random.uniform(jax.random.fold_in(own, dim), (parts,), jnp.float32, smallest / len(cuts), largest / len(cuts)))
        factor_of = factor_of * jnp.repeat(draws, extent[dim] // parts).reshape([-1 if axis == dim else 1 for axis in range(len(extent))])
    return factor_of


def scatter_about(key, shape, deviation, reach, shards=(), kind=jnp.bfloat16):
    result = deviation * jax.random.normal(key, shape, jnp.float32)
    if shards:
        result = result * steps_of(key, shape, shards, -0.22, 0.18)
    return jnp.clip(result, -reach, reach).astype(kind)


def setup_inputs(seed: int = 0) -> dict:
    seeds = jax.random.split(jax.random.key(seed), 6)
    cotangent = scatter_about(seeds[0], (TOKENS, D), 0.25, 4.0, ((0, 128),))
    routes = draw_routes(jax.random.fold_in(seeds[5], 71), 0)
    gates = jnp.clip(jnp.exp(math.log(1.0) - 2.9957323 * jax.random.uniform(seeds[2], (TOKENS, TOPK), jnp.float32) ** steps_of(seeds[2], (TOKENS, TOPK), ((0, 128),), -0.2, 0.2)), 0.05, 1.0)
    pre_act = scatter_about(seeds[3], (TOKENS, TOPK, 2 * HID), 1.0, 6.0, ((0, 128),))
    down_weight = scatter_about(seeds[4], (EXPERTS, HID, D), HID ** -0.5, 0.1875, ((0, 32),))
    return {"cotangent": cotangent, "routes": routes, "gates": gates, "pre_act": pre_act, "down_weight": down_weight}


def swish_terms(pre_rows):
    gate_pre = pre_rows[:, :HID].astype(jnp.float32)
    up_pre = pre_rows[:, HID:].astype(jnp.float32)
    return gate_pre, up_pre, jax.nn.sigmoid(gate_pre)


def compact(selected, offset, out_width, sentinel):
    position = (jnp.cumsum(selected.astype(jnp.int32)) - 1).astype(jnp.int32)
    target = jnp.where(selected, position, out_width).astype(jnp.int32)
    source = (offset + jnp.arange(selected.shape[0], dtype=jnp.int32)).astype(jnp.int32)
    return jnp.full((out_width,), sentinel, jnp.int32).at[target].set(source, mode="drop")


def expert_rows(slot_index, weight, cotangent, gates_flat, pre_flat):
    total_slots = gates_flat.shape[0]
    is_valid = slot_index < total_slots
    safe_index = jnp.minimum(slot_index, total_slots - 1).astype(jnp.int32)
    token_index = (safe_index // TOPK).astype(jnp.int32)
    gate_pre, up_pre, sigmoid_gate = swish_terms(pre_flat[safe_index])
    activation = jnp.where(is_valid[:, None], gate_pre * sigmoid_gate * up_pre, 0.0).astype(jnp.bfloat16)
    scaled = jnp.where(is_valid[:, None], gates_flat[safe_index][:, None] * cotangent[token_index].astype(jnp.float32), 0.0).astype(jnp.bfloat16)
    hidden_grad = jnp.dot(scaled, weight.T, preferred_element_type=jnp.float32).astype(jnp.bfloat16)
    widened = hidden_grad.astype(jnp.float32)
    gate_part = widened * up_pre * sigmoid_gate * (1.0 + gate_pre * (1.0 - sigmoid_gate))
    up_part = widened * gate_pre * sigmoid_gate
    grad_rows = jnp.concatenate([gate_part, up_part], axis=1).astype(jnp.bfloat16)
    outer_sum = jnp.dot(activation.T, scaled, preferred_element_type=jnp.float32)
    return grad_rows, outer_sum


def rounded(values):
    return lax.optimization_barrier(values.astype(jnp.bfloat16)).astype(jnp.float32)


def reference(cotangent, routes, gates, pre_act, down_weight):
    total_slots = TOKENS * TOPK
    flat_routes = routes.reshape(total_slots).astype(jnp.int32)
    gates_flat = gates.reshape(total_slots)
    pre_flat = pre_act.reshape(total_slots, 2 * HID)
    expert_ids = jnp.arange(EXPERTS, dtype=jnp.int32)
    counts = jnp.sum((flat_routes[:, None] == expert_ids[None, :]).astype(jnp.int32), axis=0)
    hot_expert = jnp.argmax(counts).astype(jnp.int32)
    group_slots = N_EP * TOK_DEV * TOPK
    device_slots = TOK_DEV * TOPK

    def cold_step(pre_grad, expert):
        weight = down_weight[expert]
        accumulated = jnp.zeros((HID, D), jnp.float32)
        for group_index in range(N_GRP):
            segment = flat_routes[group_index * group_slots:(group_index + 1) * group_slots]
            chosen = (segment == expert) & (expert != hot_expert)
            slot_index = compact(chosen, group_index * group_slots, N_EP * CAP, total_slots)
            grad_rows, outer_sum = expert_rows(slot_index, weight, cotangent, gates_flat, pre_flat)
            accumulated = accumulated + rounded(outer_sum)
            pre_grad = pre_grad.at[slot_index].set(grad_rows, mode="drop")
        return pre_grad, accumulated.astype(jnp.bfloat16)

    initial = jnp.zeros((total_slots, 2 * HID), jnp.bfloat16)
    pre_grad, cold_grads = lax.scan(cold_step, initial, expert_ids)
    hot_weight = down_weight[hot_expert]

    def hot_step(loop_state, device):
        grad_table, accumulated = loop_state
        segment = lax.dynamic_slice_in_dim(flat_routes, (device * device_slots).astype(jnp.int32), device_slots)
        chosen = segment == hot_expert
        slot_index = compact(chosen, device * device_slots, HOT_ROWS, total_slots)
        grad_rows, outer_sum = expert_rows(slot_index, hot_weight, cotangent, gates_flat, pre_flat)
        grad_table = grad_table.at[slot_index].set(grad_rows, mode="drop")
        return (grad_table, accumulated + rounded(outer_sum)), None

    hot_total = jnp.zeros((HID, D), jnp.float32)
    for group_index in range(N_GRP):
        devices = (group_index * N_EP + jnp.arange(N_EP, dtype=jnp.int32)).astype(jnp.int32)
        (pre_grad, group_total), _ = lax.scan(hot_step, (pre_grad, jnp.zeros((HID, D), jnp.float32)), devices)
        hot_total = hot_total + rounded(group_total)
    weight_grad = cold_grads.at[hot_expert].set(hot_total.astype(jnp.bfloat16))
    return pre_grad.reshape(TOKENS, TOPK, 2 * HID), weight_grad
```

```python
import functools

import jax
import jax.numpy as jnp
from jax import lax
from jax.experimental import pallas as pl
from jax.experimental.pallas import tpu as pltpu
from jax.sharding import PartitionSpec as P

MESH = pl.DeviceIdType.MESH
BF = jnp.bfloat16
F32 = jnp.float32

TOK = 128
TOPK = 4
SLOT = TOK * TOPK
HID = 1024
D = 3584
CAP = 20
NX, NZ = 4, 4
NJ = 8
NQ = 4
DQ = D // NQ
ROW = NX * CAP
COLD = NJ * ROW
HALF = D // 2


def dot(a, b, dims=((1,), (0,))):
    return lax.dot_general(a, b, (dims, ((), ())), preferred_element_type=F32)


NN = ((1,), (0,))
NT = ((1,), (1,))
TN = ((0,), (0,))


def iota(shape, dim):
    return lax.broadcasted_iota(jnp.int32, shape, dim)


def onehot(flag):
    return flag.astype(F32).astype(BF)


def main_kernel(
    cot, meta, rnat, pre, w,
    hid, wg,
    cg, ch, mg, pa, wq,
    ohx, ohg, pm, gc, gh,
    acts, actx, actp, actr,
    s, sr, hacc, hgx, ret,
    wgs, cr, ys, yr,
    a1r, a2s, a2r, a3s, a3r, ags, wh,
    aht, at, hht, hhs, hhacc, sh, hp, rsb, gp, g1, g2, g3,
    ssem, rsem, lsem,
):
    g, e = lax.axis_index("grp"), lax.axis_index("ep")
    yl, c = g // 2, g % 2
    x, yh, z = e // 8, (e // 4) % 2, e % 4

    def dev(dx=0, dyh=0, dz=0, dyl=0, dc=0):
        return (
            ((yl + dyl) % 2) * 2 + (c + dc) % 2,
            (((x + dx) % 4) * 2 + (yh + dyh) % 2) * 4 + (z + dz) % 4,
        )

    counts = [0, 0]

    def remote(src, dst, **to):
        k = counts[0]
        counts[0] += 1
        cp = pltpu.make_async_remote_copy(
            src_ref=src, dst_ref=dst, send_sem=ssem.at[k], recv_sem=rsem.at[k],
            device_id=dev(**to), device_id_type=MESH,
        )
        cp.start()
        return cp

    def here(src, dst):
        k = counts[1]
        counts[1] += 1
        cp = pltpu.make_async_copy(src, dst, lsem.at[k])
        cp.start()
        return cp

    sent = []

    def arrived(copies):
        for cp in copies:
            cp.wait_recv()
        sent.extend(copies)

    def left(copies):
        gone = [id(cp) for cp in copies]
        sent[:] = [cp for cp in sent if id(cp) not in gone]
        for cp in copies:
            cp.wait_send()

    def cols(q):
        return pl.ds(q * DQ, DQ)

    peers = [dict(dx=d) for d in range(1, 4)] + [dict(dx=d, dc=1) for d in range(4)]
    peers += [
        dict(dyh=a, dyl=b, dz=d)
        for a in range(2) for b in range(2) for d in range(4) if a or b or d
    ]
    barrier = pltpu.get_barrier_semaphore()
    for to in peers:
        pl.semaphore_signal(barrier, inc=1, device_id=dev(**to), device_id_type=MESH)
    own_cot = [here(cot.at[:, cols(q)], cg.at[q, pl.ds(x * TOK, TOK)]) for q in range(NQ)]
    pa_copy = here(pre, pa)
    pl.semaphore_wait(barrier, len(peers))

    meta_cp = [remote(meta, mg.at[x], dx=d) for d in range(1, 4)]
    meta_cp += [remote(meta, mg.at[4 + x], dx=d, dc=1) for d in range(4)]
    cot_cp = []
    for q in range(NQ):
        cot_cp.append([
            remote(cot.at[:, cols(q)], cg.at[q, pl.ds(x * TOK, TOK)], dx=d) for d in (1, 3, 2)
        ])
    base = 512 * yl + 256 * c
    a1_cp = []
    for d in range(1, 4):
        zt = (z + d) % 4
        for xt in range(NX):
            a1_cp.append(remote(w.at[pl.ds(base + 64 * xt + 16 * zt, 16)], a1r.at[z, xt], dz=d))
    a1_own = [
        here(w.at[pl.ds(base + 64 * xt + 16 * z, 16)], a1r.at[z, xt]) for xt in range(NX)
    ]
    w_copy = [here(w.at[:, cols(q)], wq.at[q]) for q in range(NQ)]
    mg[x] = meta[...]

    rn = rnat[...]
    eid = iota((32, SLOT), 0).astype(F32)
    member = (rn == eid).astype(F32)
    tri = onehot(iota((SLOT, SLOT), 0) < iota((SLOT, SLOT), 1))
    rank = dot(member.astype(BF), tri)
    hotv = (jnp.sum(member, axis=1, keepdims=True) >= 64.0).astype(F32)
    token = lax.shift_right_logical(iota((32, SLOT), 1), 2).astype(F32)
    place = (1.0 - hotv) * (eid * CAP + rank) + hotv * (COLD + token)
    key = jnp.sum(member * place, axis=0, keepdims=True)
    for i in range((COLD + TOK) // 128):
        ohx[pl.ds(i * 128, 128), :] = onehot(iota((128, SLOT), 0).astype(F32) + i * 128.0 == key)
    e1 = iota((32, 1), 0)

    def hot_is(flag):
        return jnp.sum(hotv * flag.astype(F32), axis=0, keepdims=True)

    hotid = jnp.sum(hotv * e1.astype(F32), axis=0, keepdims=True)
    hot_x = [hot_is(lax.shift_right_logical(e1, 3) == k) for k in range(4)]
    hot_z = [hot_is((e1 & 3) == k) for k in range(4)]
    hot_y = [hot_is((lax.shift_right_logical(e1, 2) & 1) == k) for k in range(2)]

    pa_copy.wait()

    def act_step(i, carry):
        rows = pa[pl.ds(i * 8, 8)].reshape(32, 2 * HID).astype(F32)
        gate, up = rows[:, :HID], rows[:, HID:]
        hid[pl.ds(pl.multiple_of(i * 32, 32), 32), :] = (
            gate * jax.nn.sigmoid(gate) * up
        ).astype(BF)
        return carry

    lax.fori_loop(0, TOK // 8, act_step, 0)

    def acts_step(i, carry):
        r = pl.ds(pl.multiple_of(i * 256, 256), 256)
        acts[r, :] = dot(ohx[r, :], hid[...]).astype(BF)
        return carry

    lax.fori_loop(0, 3, acts_step, 0)
    actx_cp = [
        remote(acts.at[pl.ds(((x + d) % 4) * 160, 160)], actx.at[pl.ds(x * 160, 160)], dx=d)
        for d in (1, 3, 2)
    ]
    actx_own = here(acts.at[pl.ds(x * 160, 160)], actx.at[pl.ds(x * 160, 160)])
    eye = onehot(iota((TOK, TOK), 0) == iota((TOK, TOK), 1))
    aht[...] = dot(acts[pl.ds(COLD, TOK), :], eye, TN).astype(BF)
    at_cp, at_own = [], []
    for cc in range(2):
        for d in range(4):
            for h in range(2):
                src = aht.at[pl.ds(512 * h + 256 * ((c + cc) % 2) + 64 * ((x + d) % 4), 64)]
                dst = at.at[pl.ds(64 * h, 64), pl.ds((cc * 4 + x) * TOK, TOK)]
                if cc or d:
                    at_cp.append(remote(src, dst, dx=d, dc=cc))
                else:
                    at_own.append(here(src, dst))

    arrived(meta_cp)
    tri1 = onehot(iota((TOK, TOK), 0) < iota((TOK, TOK), 1))
    ej = (iota((NJ, TOK), 0) + 8 * x).astype(F32)
    keys, gates8 = [], []
    for b in range(NX):
        m = mg[b]
        hit = [(m[k:k + 1] == ej) for k in range(TOPK)]
        mem8 = sum(f.astype(F32) for f in hit)
        gates8.append(sum(jnp.where(hit[k], m[4 + k:5 + k], 0.0) for k in range(TOPK)))
        rank8 = dot(mem8.astype(BF), tri1)
        mem8 = mem8 * (ej != hotid).astype(F32)
        keys.append(jnp.where(mem8 > 0, rank8 + CAP * b, -1.0))
    keys = jnp.concatenate(keys, axis=1)
    gates8 = jnp.concatenate(gates8, axis=1)
    rows80 = iota((ROW, SLOT), 0).astype(F32)
    for j in range(NJ):
        flag = rows80 == keys[j:j + 1]
        ohg[pl.ds(j * ROW, ROW), :] = onehot(flag)
        col = jnp.sum(jnp.where(flag, gates8[j:j + 1], 0.0), axis=1, keepdims=True)
        gc[pl.ds(j * ROW, ROW), :] = jnp.broadcast_to(col, (ROW, 128))
    diag = iota((TOK, TOK), 0) == iota((TOK, TOK), 1)
    for b in range(2 * NX):
        m = mg[b]
        row = sum(jnp.where(m[k:k + 1] == hotid, m[4 + k:5 + k], 0.0) for k in range(TOPK))
        col = jnp.sum(jnp.where(diag, row, 0.0), axis=1, keepdims=True)
        gh[pl.ds(b * TOK, TOK), :] = jnp.broadcast_to(col, (TOK, 128))
    o = iota((COLD, 128), 0)
    oj = sum((o >= ROW * k).astype(jnp.int32) for k in range(1, NJ))
    orem = o - ROW * oj
    ob = sum((orem >= CAP * k).astype(jnp.int32) for k in range(1, NX))
    want = ob * 160 + oj * CAP + (orem - CAP * ob)
    for k in range(COLD // 128):
        pm[:, pl.ds(k * 128, 128)] = onehot(want == iota((COLD, 128), 1) + k * 128)

    jme = yh * 4 + z
    zy = [(0, 1), (0, 3), (1, 0), (0, 2), (1, 1), (1, 3), (1, 2)]

    def jat(a, d):
        return ((yh + a) % 2) * 4 + (z + d) % 4

    def spread(src, dst):
        cps = [
            remote(src.at[pl.ds(jat(a, d) * ROW, ROW)], dst.at[pl.ds(jme * ROW, ROW)],
                   dyh=a, dyl=a, dz=d)
            for a, d in zy
        ]
        own = here(src.at[pl.ds(jme * ROW, ROW)], dst.at[pl.ds(jme * ROW, ROW)])
        return cps, own

    def gather_piece(q):
        own_cot[q].wait()
        arrived(cot_cp[q])

        def step(i, carry):
            r = pl.ds(pl.multiple_of(i * 320, 320), 320)
            rows = dot(ohg[r, :], cg[q]) * gc[r, 0:1]
            s[q, r, :] = rows.astype(BF)
            return carry

        lax.fori_loop(0, 2, step, 0)
        sr_cp = spread(s.at[q], sr.at[q])
        return sr_cp, remote(cg.at[q], ch.at[q], dc=1)

    sr_cp, ch_cp = [], []

    def piece(q):
        a, b = gather_piece(q)
        sr_cp.append(a)
        ch_cp.append(b)

    piece(0)
    actx_own.wait()
    arrived(actx_cp)

    def actp_step(i, carry):
        r = pl.ds(pl.multiple_of(i * 320, 320), 320)
        actp[r, :] = dot(pm[r, :], actx[...]).astype(BF)
        return carry

    lax.fori_loop(0, 2, actp_step, 0)
    actr_cp, actr_own = spread(actp, actr)

    for cp in a1_own:
        cp.wait()
    arrived(a1_cp)
    for xt in range(NX):
        a2s[xt] = sum(a1r[k, xt].astype(F32) * hot_z[k] for k in range(4)).astype(BF)
    a2_cp = [remote(a2s.at[(x + d) % 4], a2r.at[x], dx=d) for d in range(1, 4)]
    a2_own = here(a2s.at[x], a2r.at[x])
    piece(1)
    a2_own.wait()
    arrived(a2_cp)
    a3s[...] = sum(a2r[k].astype(F32) * hot_x[k] for k in range(4)).astype(BF)
    a3_cp = remote(a3s, a3r, dyh=1)
    piece(2)
    arrived([a3_cp])
    mine = hot_y[0] * (yh == 0).astype(F32) + hot_y[1] * (yh == 1).astype(F32)
    ags[...] = (a3s[...].astype(F32) * mine + a3r[...].astype(F32) * (1.0 - mine)).astype(BF)
    wh_slot = wh.at[pl.ds(yl * 64 + z * 16, 16)]
    wh_cp = [
        remote(ags, wh_slot, dyl=b, dz=d) for b in range(2) for d in range(4) if b or d
    ]
    wh_own = here(ags, wh_slot)
    piece(3)

    for cp in at_own:
        cp.wait()
    arrived(at_cp)
    wh_own.wait()
    arrived(wh_cp)
    for q in range(NQ):
        arrived([ch_cp[q]])
        for b in range(NX):
            r, t = pl.ds(b * TOK, TOK), pl.ds((4 + b) * TOK, TOK)
            sh[r, :] = (cg[q, r, :].astype(F32) * gh[r, 0:1]).astype(BF)
            sh[t, :] = (ch[q, r, :].astype(F32) * gh[t, 0:1]).astype(BF)
        hp[:, cols(q)] = dot(at[...], sh[...]).astype(BF)
        part = dot(wh[:, cols(q)], sh[...], NT)
        hhacc[...] = part if q == 0 else hhacc[...] + part
    hhs[...] = hhacc[...].astype(BF)
    hh_cp, hh_own = [], []
    for cc in range(2):
        for d in range(4):
            for h in range(2):
                src = hhs.at[pl.ds(64 * h, 64), pl.ds((cc * 4 + (x + d) % 4) * TOK, TOK)]
                dst = hht.at[pl.ds(512 * h + 256 * c + 64 * x, 64)]
                if cc or d:
                    hh_cp.append(remote(src, dst, dx=d, dc=cc))
                else:
                    hh_own.append(here(src, dst))
    rs_cp = []
    k = 1
    for a in range(2):
        for b in range(2):
            for d in range(4):
                src = hp.at[
                    pl.ds(((yl + b) % 2) * 64 + ((z + d) % 4) * 16, 16),
                    pl.ds(((yh + a) % 2) * HALF, HALF),
                ]
                if a or b or d:
                    rs_cp.append(remote(src, rsb.at[k], dyh=a, dyl=b, dz=d))
                    k += 1
                else:
                    rs_own = here(src, rsb.at[0])

    actr_own.wait()
    arrived(actr_cp)
    yr_cp = []
    for q in range(NQ):
        w_copy[q].wait()
        sr_cp[q][1].wait()
        arrived(sr_cp[q][0])

        def wg_step(i, carry):
            r = pl.ds(pl.multiple_of(i * 256, 256), 256)
            wgs[r, :] = dot(actr[:, r], sr[q], TN).astype(BF)
            return carry

        lax.fori_loop(0, 4, wg_step, 0)
        cr_cp = [
            remote(wgs.at[pl.ds(512 * h + 256 * ((c + 1) % 2), 256)], cr.at[q % 2, h], dc=1)
            for h in range(2)
        ]

        def dg_step(i, carry):
            r = pl.ds(pl.multiple_of(i * 256, 256), 256)
            part = dot(sr[q], wq[q, r, :], NT)
            hacc[:, r] = part if q == 0 else hacc[:, r] + part
            return carry

        lax.fori_loop(0, 4, dg_step, 0)
        for cp in cr_cp:
            cp.wait()
        there, stay = (yl + 1) % 2, yl
        if q >= 2:
            yr_cp[q - 2].wait_send()
        ys[q % 2] = (
            wgs[pl.ds(512 * there + 256 * c, 256), :].astype(F32)
            + cr[q % 2, there].astype(F32)
        ).astype(BF)
        yr_cp.append(remote(ys.at[q % 2], yr.at[q], dyl=1))
        wg[:, cols(q)] = (
            wgs[pl.ds(512 * stay + 256 * c, 256), :].astype(F32)
            + cr[q % 2, stay].astype(F32)
        ).astype(BF)
    left(actx_cp)
    hg = acts

    def hg_step(i, carry):
        r = pl.ds(pl.multiple_of(i * 128, 128), 128)
        hg[r, :] = hacc[r, :].astype(BF)
        return carry

    lax.fori_loop(0, 5, hg_step, 0)
    hgx_cp, hgx_own = spread(hg, hgx)

    rs_own.wait()
    arrived(rs_cp)
    gp[...] = sum(rsb[k].astype(F32) for k in range(16)).astype(BF)
    g1_cp = [remote(gp, g1.at[z], dz=d) for d in range(1, 4)]
    g1_own = here(gp, g1.at[z])

    left(actr_cp)
    hgx_own.wait()
    arrived(hgx_cp)
    hgp = actp

    for i in range(5):
        r = pl.ds(i * 128, 128)
        hgp[r, :] = dot(pm[:, r], hgx[...], TN).astype(BF)
    ret_cp = [
        remote(hgp.at[pl.ds(((x + d) % 4) * 160, 160)], ret.at[pl.ds(x * 160, 160)], dx=d)
        for d in (1, 3, 2)
    ]
    ret_own = here(hgp.at[pl.ds(x * 160, 160)], ret.at[pl.ds(x * 160, 160)])

    g1_own.wait()
    arrived(g1_cp)
    g2_cp = remote(g1, g2.at[yh], dyh=1)
    g2_own = here(g1, g2.at[yh])
    for cp in hh_own:
        cp.wait()
    arrived(hh_cp)
    ret[pl.ds(COLD, TOK), :] = dot(eye, hht[...], NT).astype(BF)
    g2_own.wait()
    arrived([g2_cp])
    g3_cp = [remote(g2, g3.at[x], dx=d) for d in (1, 3, 2)]
    g3_own = here(g2, g3.at[x])

    ret_own.wait()
    arrived(ret_cp)

    def out_step(i, carry):
        r = pl.ds(pl.multiple_of(i * 256, 256), 256)
        hid[:, r] = dot(ohx[...], ret[:, r], TN).astype(BF)
        return carry

    lax.fori_loop(0, 4, out_step, 0)

    for q in range(NQ):
        yr_cp[q].wait_recv()
        if q >= 2:
            sent.append(yr_cp[q])
        wg[:, cols(q)] = (wg[:, cols(q)].astype(F32) + yr[q].astype(F32)).astype(BF)
    g3_own.wait()
    arrived(g3_cp)
    own = (e1 == e).astype(F32)
    is_hot = jnp.sum(own * hotv, axis=0, keepdims=True)
    for xt in range(NX):
        for h in range(2):
            for zt in range(NZ):
                r, k = pl.ds(64 * xt + 16 * zt, 16), pl.ds(h * HALF, HALF)
                wg[r, k] = (
                    wg[r, k].astype(F32) * (1.0 - is_hot) + g3[xt, h, zt].astype(F32) * is_hot
                ).astype(BF)
    for cp in sent:
        cp.wait_send()


def vm(*shape, dtype=BF):
    return pltpu.VMEM(shape, dtype)


def run_main(cot, meta, rnat, pre, w):
    anyw = pl.BlockSpec(memory_space=pl.ANY)
    vmem = pl.BlockSpec(memory_space=pltpu.VMEM)
    scratch = [
        vm(NQ, SLOT, DQ), vm(NQ, SLOT, DQ), vm(8, 8, 128, dtype=F32), vm(TOK, TOPK, 2 * HID),
        vm(NQ, HID, DQ),
        vm(COLD + TOK, SLOT), vm(COLD, SLOT), vm(COLD, COLD), vm(COLD, 128, dtype=F32),
        vm(8 * TOK, 128, dtype=F32),
        vm(COLD + TOK, HID), vm(COLD, HID), vm(COLD, HID), vm(COLD, HID),
        vm(NQ, COLD, DQ), vm(NQ, COLD, DQ), vm(COLD, HID, dtype=F32), vm(COLD, HID),
        vm(COLD + TOK, HID),
        vm(HID, DQ), vm(2, 2, 256, DQ), vm(2, 256, DQ), vm(NQ, 256, DQ),
        vm(4, 4, 16, D), vm(4, 16, D), vm(4, 16, D), vm(16, D), vm(16, D), vm(16, D),
        vm(128, D),
        vm(HID, TOK), vm(128, 8 * TOK), vm(HID, TOK), vm(128, 8 * TOK),
        vm(128, 8 * TOK, dtype=F32), vm(8 * TOK, DQ), vm(128, D), vm(16, 16, HALF),
        vm(16, HALF), vm(4, 16, HALF), vm(2, 4, 16, HALF), vm(4, 2, 4, 16, HALF),
        pltpu.SemaphoreType.DMA((192,)), pltpu.SemaphoreType.DMA((192,)),
        pltpu.SemaphoreType.DMA((40,)),
    ]
    return pl.pallas_call(
        main_kernel,
        out_shape=(
            jax.ShapeDtypeStruct((SLOT, HID), BF),
            jax.ShapeDtypeStruct((256, D), BF),
        ),
        in_specs=[anyw, vmem, vmem, anyw, anyw],
        out_specs=(vmem, vmem),
        scratch_shapes=scratch,
        compiler_params=pltpu.CompilerParams(
            collective_id=0, has_side_effects=True, vmem_limit_bytes=60 * 1024 * 1024
        ),
        cost_estimate=pl.CostEstimate(
            flops=22 * 10**9, bytes_accessed=16 * 10**6, transcendentals=10**6
        ),
    )(cot, meta, rnat, pre, w)


def grad_kernel(h, p, o):
    n = h.shape[0]
    back = h[...].astype(F32)
    rows = p[...].reshape(n, 2 * HID).astype(F32)
    gate, up = rows[:, :HID], rows[:, HID:]
    sig = jax.nn.sigmoid(gate)
    left = back * up * sig * (1.0 + gate * (1.0 - sig))
    right = back * gate * sig
    o[:, :, :HID] = left.astype(BF).reshape(n // TOPK, TOPK, HID)
    o[:, :, HID:] = right.astype(BF).reshape(n // TOPK, TOPK, HID)


def run_grad(hidden, pre):
    n = 16
    return pl.pallas_call(
        grad_kernel,
        grid=(TOK // n,),
        out_shape=jax.ShapeDtypeStruct((TOK, TOPK, 2 * HID), BF),
        in_specs=[
            pl.BlockSpec((n * TOPK, HID), lambda i: (i, 0)),
            pl.BlockSpec((n, TOPK, 2 * HID), lambda i: (i, 0, 0)),
        ],
        out_specs=pl.BlockSpec((n, TOPK, 2 * HID), lambda i: (i, 0, 0)),
        compiler_params=pltpu.CompilerParams(vmem_limit_bytes=24 * 1024 * 1024),
    )(hidden, pre)


def local(cotangent, routes, gates, pre_act, down_weight):
    meta = jnp.concatenate([routes.astype(F32).T, gates.T], axis=0)
    rnat = routes.astype(F32).reshape(1, SLOT)
    hidden, weight = run_main(cotangent, meta, rnat, pre_act, down_weight[0])
    return run_grad(hidden, pre_act), weight[None]


def solution(mesh):
    in_specs = (
        P(("grp", "ep"), None),
        P(("grp", "ep"), None),
        P(("grp", "ep"), None),
        P(("grp", "ep"), None, None),
        P("ep", None, None),
    )
    out_specs = (P(("grp", "ep"), None, None), P("ep", "grp", None))
    return jax.shard_map(local, mesh=mesh, in_specs=in_specs, out_specs=out_specs, check_vma=False)
```

```python
import functools

import jax
import jax.numpy as jnp
from jax import lax
from jax.experimental import pallas as pl
from jax.experimental.pallas import tpu as pltpu
from jax.sharding import PartitionSpec as P

MESH = pl.DeviceIdType.MESH
BF = jnp.bfloat16
F32 = jnp.float32

TOK = 128
TOPK = 4
SLOT = TOK * TOPK
HID = 1024
D = 3584
CAP = 20
NX, NZ = 4, 4
NJ = 8
NQ = 4
DQ = D // NQ
ROW = NX * CAP
COLD = NJ * ROW
HALF = D // 2
HALFHID = HID // 2


def dot(a, b, dims=((1,), (0,))):
    return lax.dot_general(a, b, (dims, ((), ())), preferred_element_type=F32)


NN = ((1,), (0,))
NT = ((1,), (1,))
TN = ((0,), (0,))


def iota(shape, dim):
    return lax.broadcasted_iota(jnp.int32, shape, dim)


def onehot(flag):
    return flag.astype(F32).astype(BF)


def main_kernel(
    cot, meta, rnat, pre, w,
    hid, wg,
    cg, ch, mg, pa, wq,
    ohx, sel, ohg, pm, px, gc,
    acts, actx, actp, actr, actb,
    s, sr, sp, hacc, hgx, ret,
    wgs, cr, ys, yr,
    a1r, a2s, a2r, a3s, a3r, ags, wh,
    ahot, aht, at, hht, hhs, hp, rsb, gp, g1, g2, g3,
    ssem, rsem, lsem,
):
    g, e = lax.axis_index("grp"), lax.axis_index("ep")
    yl, c = g // 2, g % 2
    x, yh, z = e // 8, (e // 4) % 2, e % 4
    us, vs = (x, z), (z, x)

    def dev(dx=0, dyh=0, dz=0, dyl=0, dc=0):
        return (
            ((yl + dyl) % 2) * 2 + (c + dc) % 2,
            (((x + dx) % 4) * 2 + (yh + dyh) % 2) * 4 + (z + dz) % 4,
        )

    def way(p, du=0, dv=0, **to):
        return dict(dx=(du, dv)[p], dz=(dv, du)[p], **to)

    counts = [0, 0]

    def remote(src, dst, **to):
        k = counts[0]
        counts[0] += 1
        cp = pltpu.make_async_remote_copy(
            src_ref=src, dst_ref=dst, send_sem=ssem.at[k], recv_sem=rsem.at[k],
            device_id=dev(**to), device_id_type=MESH,
        )
        cp.start()
        return cp

    def here(src, dst):
        k = counts[1]
        counts[1] += 1
        cp = pltpu.make_async_copy(src, dst, lsem.at[k])
        cp.start()
        return cp

    sent = []

    def arrived(copies):
        for cp in copies:
            cp.wait_recv()
        sent.extend(copies)

    def left(copies):
        gone = [id(cp) for cp in copies]
        sent[:] = [cp for cp in sent if id(cp) not in gone]
        for cp in copies:
            cp.wait_send()

    def cols(q):
        return pl.ds(q * DQ, DQ)

    def half(p):
        return pl.ds(p * HALF, HALF)

    def hh(p):
        return pl.ds(p * HALFHID, HALFHID)

    peers = set()
    for p in range(2):
        for d in range(4):
            for a in range(2):
                for b in range(2):
                    peers.add(tuple(sorted(way(p, dv=d, dyh=a, dyl=b, dc=0).items())))
            for cc in range(2):
                peers.add(tuple(sorted(way(p, du=d, dyh=0, dyl=0, dc=cc).items())))
    peers = [dict(t) for t in sorted(peers) if any(v for _, v in t)]
    barrier = pltpu.get_barrier_semaphore()
    for to in peers:
        pl.semaphore_signal(barrier, inc=1, device_id=dev(**to), device_id_type=MESH)
    ORDER = (0, 2, 1, 3)
    own_cot = {}
    for q in ORDER:
        own_cot[q] = here(cot.at[:, cols(q)], cg.at[q, pl.ds(us[q // 2] * TOK, TOK)])
    NP = 4
    pt = TOK // NP
    pa_copy = [here(pre.at[pl.ds(i * pt, pt)], pa.at[i]) for i in range(2)]
    pl.semaphore_wait(barrier, len(peers))

    cot_cp = {}

    def send_cot(q):
        p = q // 2
        cot_cp[q] = [
            remote(cot.at[:, cols(q)], cg.at[q, pl.ds(us[p] * TOK, TOK)], **way(p, du=d))
            for d in (1, 3, 2)
        ]

    meta_cp = []
    for p in range(2):
        for cc in range(2):
            for d in range(4):
                if cc or d:
                    meta_cp.append(remote(meta, mg.at[p, cc * 4 + us[p]], **way(p, du=d, dc=cc)))
    send_cot(0)
    send_cot(2)
    for p in range(2):
        mg[p, us[p]] = meta[...]

    rn = rnat[...]
    ei = iota((32, SLOT), 0)
    eid = ei.astype(F32)
    member = (rn == eid).astype(F32)
    tri = onehot(iota((SLOT, SLOT), 0) < iota((SLOT, SLOT), 1))
    rank = dot(member.astype(BF), tri)
    hotv = (jnp.sum(member, axis=1, keepdims=True) >= 64.0).astype(F32)
    token = lax.shift_right_logical(iota((32, SLOT), 1), 2).astype(F32)
    turned = ((ei & 3) * 8 + (ei & 4) + lax.shift_right_logical(ei, 3)).astype(F32)
    cold = member * (1.0 - hotv)
    for p in range(2):
        order = (eid, turned)[p]
        key = jnp.sum(cold * (order * CAP + rank) - (member - cold), axis=0, keepdims=True)
        for i in range(COLD // 128):
            ohx[p, pl.ds(i * 128, 128), :] = onehot(
                iota((128, SLOT), 0).astype(F32) + i * 128.0 == key
            )
    key = jnp.sum(member * hotv * (token + 1.0), axis=0, keepdims=True) - 1.0
    sel[...] = onehot(iota((128, SLOT), 0).astype(F32) == key)
    e1 = iota((32, 1), 0)

    def hot_is(flag):
        return jnp.sum(hotv * flag.astype(F32), axis=0, keepdims=True)

    hotid = jnp.sum(hotv * e1.astype(F32), axis=0, keepdims=True)
    hot_x = [hot_is(lax.shift_right_logical(e1, 3) == k) for k in range(4)]
    hot_z = [hot_is((e1 & 3) == k) for k in range(4)]
    hot_y = [hot_is((lax.shift_right_logical(e1, 2) & 1) == k) for k in range(2)]
    hot_u, hot_v = (hot_x, hot_z), (hot_z, hot_x)

    send_cot(1)
    send_cot(3)
    a1_cp, a1_own = [], []
    for p in range(2):
        a1_cp.append([
            remote(w.at[yl, c, :, (vs[p] + d) % 4, :, half(p)], a1r.at[p, vs[p]], **way(p, dv=d))
            for d in (1, 3, 2)
        ])
        a1_own.append(here(w.at[yl, c, :, vs[p], :, half(p)], a1r.at[p, vs[p]]))
    w_copy = {q: here(w.at[:, :, :, :, :, cols(q)], wq.at[q]) for q in ORDER}

    for i in range(NP):
        pa_copy[i].wait()

        def act_step(j, carry):
            rows = pa[i % 2, pl.ds(j * 8, 8)].reshape(32, 2 * HID).astype(F32)
            gate, up = rows[:, :HID], rows[:, HID:]
            hid[pl.ds(pl.multiple_of(i * pt * 4 + j * 32, 32), 32), :] = (
                gate * jax.nn.sigmoid(gate) * up
            ).astype(BF)
            return carry

        lax.fori_loop(0, pt // 8, act_step, 0)
        if i + 2 < NP:
            pa_copy.append(here(pre.at[pl.ds((i + 2) * pt, pt)], pa.at[i % 2]))

    actx_cp, actx_own = [], []
    for p in range(2):

        def acts_step(i, carry):
            r = pl.ds(pl.multiple_of(i * 320, 320), 320)
            acts[p, r, :] = dot(ohx[p, r, :], hid[:, hh(p)]).astype(BF)
            return carry

        lax.fori_loop(0, 2, acts_step, 0)
        u = us[p]
        actx_cp.append([
            remote(acts.at[p, pl.ds(((u + d) % 4) * 160, 160)], actx.at[p, pl.ds(u * 160, 160)],
                   **way(p, du=d))
            for d in (1, 3, 2)
        ])
        actx_own.append(here(acts.at[p, pl.ds(u * 160, 160)], actx.at[p, pl.ds(u * 160, 160)]))
    ahot[...] = dot(sel[...], hid[...]).astype(BF)
    eye = onehot(iota((TOK, TOK), 0) == iota((TOK, TOK), 1))
    aht[...] = dot(ahot[...], eye, TN).astype(BF).reshape(2, HID // 2, TOK)

    def ring_part(p, d, cc):
        return pl.ds(256 * ((c + cc) % 2) + 64 * ((us[p] + d) % 4), 64)

    at_cp, at_own = [], []
    for p in range(2):
        at_cp.append([])
        for cc in range(2):
            for d in range(4):
                src = aht.at[:, ring_part(p, d, cc), :]
                dst = at.at[p, :, :, pl.ds((cc * 4 + us[p]) * TOK, TOK)]
                if cc or d:
                    at_cp[p].append(remote(src, dst, **way(p, du=d, dc=cc)))
                else:
                    at_own.append(here(src, dst))

    arrived(meta_cp)
    tri1 = onehot(iota((TOK, TOK), 0) < iota((TOK, TOK), 1))
    i8 = iota((NJ, TOK), 0)
    rows80 = iota((ROW, SLOT), 0).astype(F32)
    for p in range(2):
        if p == 0:
            ej = (i8 + 8 * x).astype(F32)
        else:
            ej = ((i8 & 3) * 8 + (i8 & 4) + z).astype(F32)
        keys, gates8 = [], []
        for b in range(NX):
            m = mg[p, b]
            hit = [(m[k:k + 1] == ej) for k in range(TOPK)]
            mem8 = sum(f.astype(F32) for f in hit)
            gates8.append(sum(jnp.where(hit[k], m[4 + k:5 + k], 0.0) for k in range(TOPK)))
            rank8 = dot(mem8.astype(BF), tri1)
            mem8 = mem8 * (ej != hotid).astype(F32)
            keys.append(jnp.where(mem8 > 0, rank8 + CAP * b, -1.0))
        keys = jnp.concatenate(keys, axis=1)
        gates8 = jnp.concatenate(gates8, axis=1)
        for j in range(NJ):
            flag = rows80 == keys[j:j + 1]
            ohg[p, pl.ds(j * ROW, ROW), :] = onehot(flag)
            col = jnp.sum(jnp.where(flag, gates8[j:j + 1], 0.0), axis=1, keepdims=True)
            gc[p, pl.ds(j * ROW, ROW), :] = jnp.broadcast_to(col, (ROW, 128))

    def spread(p, src, dst):
        v = vs[p]
        cps = [
            remote(
                src.at[pl.ds((((yh + a) % 2) * 4 + (v + d) % 4) * ROW, ROW)],
                dst.at[pl.ds((yh * 4 + v) * ROW, ROW)], **way(p, dv=d, dyh=a, dyl=a),
            )
            for a, d in ((0, 1), (0, 3), (1, 0), (0, 2), (1, 1), (1, 3), (1, 2))
        ]
        own = pl.ds((yh * 4 + v) * ROW, ROW)
        return cps, here(src.at[own], dst.at[own])

    sr_cp, ch_cp = {}, {}

    def piece(q):
        p = q // 2
        own_cot[q].wait()
        arrived(cot_cp[q])

        def step(i, carry):
            r = pl.ds(pl.multiple_of(i * 320, 320), 320)
            s[q, r, :] = (dot(ohg[p, r, :], cg[q]) * gc[p, r, 0:1]).astype(BF)
            return carry

        lax.fori_loop(0, 2, step, 0)
        sr_cp[q] = spread(p, s.at[q], sr.at[q])
        ch_cp[q] = remote(cg.at[q], ch.at[q], dc=1)

    piece(0)
    piece(2)
    o = iota((COLD, 128), 0)
    oj = sum((o >= ROW * k).astype(jnp.int32) for k in range(1, NJ))
    orem = o - ROW * oj
    ob = sum((orem >= CAP * k).astype(jnp.int32) for k in range(1, NX))
    want = ob * 160 + oj * CAP + (orem - CAP * ob)
    for k in range(COLD // 128):
        pm[:, pl.ds(k * 128, 128)] = onehot(want == iota((COLD, 128), 1) + k * 128)
    o = iota((4 * ROW, 4 * ROW), 0)
    oj = sum((o >= ROW * k).astype(jnp.int32) for k in range(1, 4))
    orem = o - ROW * oj
    ob = sum((orem >= CAP * k).astype(jnp.int32) for k in range(1, NX))
    px[...] = onehot(ob * ROW + oj * CAP + (orem - CAP * ob) == iota((4 * ROW, 4 * ROW), 1))

    def turn(src, dst):
        for k in range(2):
            r = pl.ds(k * 4 * ROW, 4 * ROW)
            dst[r, :] = dot(px[...], src[r, :]).astype(BF)

    actr_cp, actr_own = [], []
    for p in range(2):
        actx_own[p].wait()
        arrived(actx_cp[p])

        def actp_step(i, carry):
            r = pl.ds(pl.multiple_of(i * 320, 320), 320)
            actp[p, r, :] = dot(pm[r, :], actx[p]).astype(BF)
            return carry

        lax.fori_loop(0, 2, actp_step, 0)
        a, b = spread(p, actp.at[p], actr.at[p])
        actr_cp.append(a)
        actr_own.append(b)

    a2_cp, a2_own, a3_cp, wh_cp, wh_own = [], [], [], [], []
    for p in range(2):
        a1_own[p].wait()
        arrived(a1_cp[p])
        for k in range(4):
            a2s[p, k] = sum(a1r[p, i, k].astype(F32) * hot_v[p][i] for i in range(4)).astype(BF)
        u = us[p]
        a2_cp.append([
            remote(a2s.at[p, (u + d) % 4], a2r.at[p, u], **way(p, du=d)) for d in (1, 3, 2)
        ])
        a2_own.append(here(a2s.at[p, u], a2r.at[p, u]))
    piece(1)
    for p in range(2):
        a2_own[p].wait()
        arrived(a2_cp[p])
        a3s[p] = sum(a2r[p, k].astype(F32) * hot_u[p][k] for k in range(4)).astype(BF)
        a3_cp.append(remote(a3s.at[p], a3r.at[p], dyh=1))
    piece(3)
    mine = hot_y[0] * (yh == 0).astype(F32) + hot_y[1] * (yh == 1).astype(F32)
    for p in range(2):
        arrived([a3_cp[p]])
        ags[p] = (
            a3s[p].astype(F32) * mine + a3r[p].astype(F32) * (1.0 - mine)
        ).astype(BF)
        slot = wh.at[p, yl, vs[p]]
        wh_cp.append([
            remote(ags.at[p], slot, **way(p, dv=d, dyl=b))
            for b in range(2) for d in range(4) if b or d
        ])
        wh_own.append(here(ags.at[p], slot))

    sh = wgs
    diag = iota((TOK, TOK), 0) == iota((TOK, TOK), 1)
    hh_cp, hh_own, rs_cp, rs_own = [], [], [], []
    for p in range(2):
        at_own[p].wait()
        arrived(at_cp[p])
        wh_own[p].wait()
        arrived(wh_cp[p])
        for i in range(2):
            q = 2 * p + i
            arrived([ch_cp[q]])
            for b in range(2 * NX):
                m = mg[p, b]
                row = sum(
                    jnp.where(m[k:k + 1] == hotid, m[4 + k:5 + k], 0.0) for k in range(TOPK)
                )
                col = jnp.sum(jnp.where(diag, row, 0.0), axis=1, keepdims=True)
                block = (cg, ch)[b // NX][q, pl.ds((b % NX) * TOK, TOK), :]
                sh[pl.ds(b * TOK, TOK), :] = (block.astype(F32) * col).astype(BF)
            hp[q] = dot(at[p].reshape(128, 8 * TOK), sh[...]).astype(BF)
            part = dot(wh[p, :, :, :, pl.ds(i * DQ, DQ)].reshape(128, DQ), sh[...], NT)
            hacc[0:128, :] = part if i == 0 else hacc[0:128, :] + part
        hhs[p] = hacc[0:128, :].astype(BF).reshape(2, 64, 8 * TOK)
        hh_cp.append([])
        for cc in range(2):
            for d in range(4):
                src = hhs.at[p, :, :, pl.ds((cc * 4 + (us[p] + d) % 4) * TOK, TOK)]
                dst = hht.at[p, :, pl.ds(256 * c + 64 * us[p], 64), :]
                if cc or d:
                    hh_cp[p].append(remote(src, dst, **way(p, du=d, dc=cc)))
                else:
                    hh_own.append(here(src, dst))
        rs_cp.append([])
        k = 1
        for a in range(2):
            for b in range(2):
                for d in range(4):
                    src = hp.at[
                        2 * p + (yh + a) % 2,
                        pl.ds(((yl + b) % 2) * 64 + ((vs[p] + d) % 4) * 16, 16),
                    ]
                    if a or b or d:
                        rs_cp[p].append(
                            remote(src, rsb.at[p, k], **way(p, dv=d, dyh=a, dyl=b))
                        )
                        k += 1
                    else:
                        rs_own.append(here(src, rsb.at[p, 0]))

    for p in range(2):
        actr_own[p].wait()
        arrived(actr_cp[p])
    turn(actr.at[1], actb)
    yr_cp = {}
    last_ys = {}
    for n, q in enumerate(ORDER):
        w_copy[q].wait()
        sr_cp[q][1].wait()
        arrived(sr_cp[q][0])
        rows = sr.at[q]
        if q >= 2:
            turn(sr.at[q], sp)
            rows = sp

        for p in range(2):
            act = (actr.at[0], actb)[p]

            def wg_step(i, carry):
                r = pl.ds(pl.multiple_of(i * 256, 256), 256)
                wgs[pl.ds(pl.multiple_of(p * HALFHID + i * 256, 256), 256), :] = dot(
                    act[:, r], rows[...], TN
                ).astype(BF)
                return carry

            lax.fori_loop(0, 2, wg_step, 0)
        cr_cp = [
            remote(wgs.at[pl.ds(512 * h + 256 * ((c + 1) % 2), 256)], cr.at[n % 2, h], dc=1)
            for h in range(2)
        ]

        for h in range(2):
            for k in range(2):
                r = pl.ds(512 * h + 256 * k, 256)
                part = dot(rows[...], wq[q, h, k].reshape(256, DQ), NT)
                hacc[:, r] = part if n == 0 else hacc[:, r] + part
        for cp in cr_cp:
            cp.wait()
        there, stay = (yl + 1) % 2, yl
        if n >= 2:
            yr_cp[ORDER[n - 2]].wait_send()
        ys[n % 2] = (
            wgs[pl.ds(512 * there + 256 * c, 256), :].astype(F32)
            + cr[n % 2, there].astype(F32)
        ).astype(BF)
        yr_cp[q] = remote(ys.at[n % 2], yr.at[q], dyl=1)
        wg[:, cols(q)] = (
            wgs[pl.ds(512 * stay + 256 * c, 256), :].astype(F32)
            + cr[n % 2, stay].astype(F32)
        ).astype(BF)
    for p in range(2):
        left(actx_cp[p])
    hg = acts
    hgx_cp, hgx_own = [], []
    for p in range(2):
        if p == 0:
            hg[0] = hacc[:, hh(0)].astype(BF)
        else:
            for k in range(2):
                r = pl.ds(k * 4 * ROW, 4 * ROW)
                hg[1, r, :] = dot(px[...], hacc[r, hh(1)].astype(BF)).astype(BF)
        a, b = spread(p, hg.at[p], hgx.at[p])
        hgx_cp.append(a)
        hgx_own.append(b)

    g1_cp, g1_own, g2_cp, g2_own, g3_cp, g3_own = [], [], [], [], [], []
    for p in range(2):
        rs_own[p].wait()
        arrived(rs_cp[p])
        gp[p] = sum(rsb[p, k].astype(F32) for k in range(16)).astype(BF)
        g1_cp.append([remote(gp.at[p], g1.at[p, vs[p]], **way(p, dv=d)) for d in (1, 3, 2)])
        g1_own.append(here(gp.at[p], g1.at[p, vs[p]]))

    hgp = actp
    ret_cp, ret_own = [], []
    for p in range(2):
        left(actr_cp[p])
        hgx_own[p].wait()
        arrived(hgx_cp[p])
        for i in range(5):
            r = pl.ds(i * 128, 128)
            hgp[p, r, :] = dot(pm[:, r], hgx[p], TN).astype(BF)
        u = us[p]
        ret_cp.append([
            remote(hgp.at[p, pl.ds(((u + d) % 4) * 160, 160)], ret.at[p, pl.ds(u * 160, 160)],
                   **way(p, du=d))
            for d in (1, 3, 2)
        ])
        ret_own.append(here(hgp.at[p, pl.ds(u * 160, 160)], ret.at[p, pl.ds(u * 160, 160)]))

    for p in range(2):
        g1_own[p].wait()
        arrived(g1_cp[p])
        g2_cp.append(remote(g1.at[p], g2.at[p, yh], dyh=1))
        g2_own.append(here(g1.at[p], g2.at[p, yh]))
    for p in range(2):
        hh_own[p].wait()
        arrived(hh_cp[p])
    ahot[...] = (
        dot(eye, hht[0].reshape(HID, TOK), NT) + dot(eye, hht[1].reshape(HID, TOK), NT)
    ).astype(BF)
    for p in range(2):
        g2_own[p].wait()
        arrived([g2_cp[p]])
        g3_cp.append([remote(g2.at[p], g3.at[p, us[p]], **way(p, du=d)) for d in (1, 3, 2)])
        g3_own.append(here(g2.at[p], g3.at[p, us[p]]))

    for p in range(2):
        ret_own[p].wait()
        arrived(ret_cp[p])
        for i in range(2):
            r, t = pl.ds(i * 256, 256), pl.ds(p * HALFHID + i * 256, 256)
            hid[:, t] = (dot(ohx[p], ret[p, :, r], TN) + dot(sel[...], ahot[:, t], TN)).astype(BF)

    for n, q in enumerate(ORDER):
        yr_cp[q].wait_recv()
        if n >= 2:
            sent.append(yr_cp[q])
        wg[:, cols(q)] = (wg[:, cols(q)].astype(F32) + yr[q].astype(F32)).astype(BF)
    own = (e1 == e).astype(F32)
    is_hot = jnp.sum(own * hotv, axis=0, keepdims=True)
    for p in range(2):
        g3_own[p].wait()
        arrived(g3_cp[p])
        for ut in range(4):
            for i in range(2):
                for vt in range(4):
                    r, k = pl.ds(64 * ut + 16 * vt, 16), cols(2 * p + i)
                    wg[r, k] = (
                        wg[r, k].astype(F32) * (1.0 - is_hot)
                        + g3[p, ut, i, vt].astype(F32) * is_hot
                    ).astype(BF)
    for cp in sent:
        cp.wait_send()


def vm(*shape, dtype=BF):
    return pltpu.VMEM(shape, dtype)


def run_main(cot, meta, rnat, pre, w):
    anyw = pl.BlockSpec(memory_space=pl.ANY)
    vmem = pl.BlockSpec(memory_space=pltpu.VMEM)
    scratch = [
        vm(NQ, SLOT, DQ), vm(NQ, SLOT, DQ), vm(2, 8, 8, 128, dtype=F32),
        vm(2, TOK // 4, TOPK, 2 * HID), vm(NQ, 2, 2, 4, 4, 16, DQ),
        vm(2, COLD, SLOT), vm(TOK, SLOT), vm(2, COLD, SLOT), vm(COLD, COLD),
        vm(4 * ROW, 4 * ROW), vm(2, COLD, 128, dtype=F32),
        vm(2, COLD, HALFHID), vm(2, COLD, HALFHID), vm(2, COLD, HALFHID), vm(2, COLD, HALFHID),
        vm(COLD, HALFHID),
        vm(NQ, COLD, DQ), vm(NQ, COLD, DQ), vm(COLD, DQ), vm(COLD, HID, dtype=F32),
        vm(2, COLD, HALFHID), vm(2, COLD, HALFHID),
        vm(HID, DQ), vm(2, 2, 256, DQ), vm(2, 256, DQ), vm(NQ, 256, DQ),
        vm(2, 4, 4, 16, HALF), vm(2, 4, 16, HALF), vm(2, 4, 16, HALF),
        vm(2, 16, HALF), vm(2, 16, HALF), vm(2, 16, HALF), vm(2, 2, 4, 16, HALF),
        vm(TOK, HID), vm(2, HID // 2, TOK), vm(2, 2, 64, 8 * TOK), vm(2, 2, HID // 2, TOK),
        vm(2, 2, 64, 8 * TOK), vm(NQ, 128, DQ),
        vm(2, 16, 16, DQ), vm(2, 16, DQ), vm(2, 4, 16, DQ), vm(2, 2, 4, 16, DQ),
        vm(2, 4, 2, 4, 16, DQ),
        pltpu.SemaphoreType.DMA((256,)), pltpu.SemaphoreType.DMA((256,)),
        pltpu.SemaphoreType.DMA((64,)),
    ]
    return pl.pallas_call(
        main_kernel,
        out_shape=(
            jax.ShapeDtypeStruct((SLOT, HID), BF),
            jax.ShapeDtypeStruct((256, D), BF),
        ),
        in_specs=[anyw, vmem, vmem, anyw, anyw],
        out_specs=(vmem, vmem),
        scratch_shapes=scratch,
        compiler_params=pltpu.CompilerParams(
            collective_id=0, has_side_effects=True, vmem_limit_bytes=61 * 1024 * 1024
        ),
        cost_estimate=pl.CostEstimate(
            flops=22 * 10**9, bytes_accessed=16 * 10**6, transcendentals=10**6
        ),
    )(cot, meta, rnat, pre, w)


def grad_kernel(h, p, o):
    n = h.shape[0]
    back = h[...].astype(F32)
    rows = p[...].reshape(n, 2 * HID).astype(F32)
    gate, up = rows[:, :HID], rows[:, HID:]
    sig = jax.nn.sigmoid(gate)
    left = back * up * sig * (1.0 + gate * (1.0 - sig))
    right = back * gate * sig
    o[:, :, :HID] = left.astype(BF).reshape(n // TOPK, TOPK, HID)
    o[:, :, HID:] = right.astype(BF).reshape(n // TOPK, TOPK, HID)


def run_grad(hidden, pre):
    n = 16
    return pl.pallas_call(
        grad_kernel,
        grid=(TOK // n,),
        out_shape=jax.ShapeDtypeStruct((TOK, TOPK, 2 * HID), BF),
        in_specs=[
            pl.BlockSpec((n * TOPK, HID), lambda i: (i, 0)),
            pl.BlockSpec((n, TOPK, 2 * HID), lambda i: (i, 0, 0)),
        ],
        out_specs=pl.BlockSpec((n, TOPK, 2 * HID), lambda i: (i, 0, 0)),
        compiler_params=pltpu.CompilerParams(vmem_limit_bytes=24 * 1024 * 1024),
    )(hidden, pre)


def local(cotangent, routes, gates, pre_act, down_weight):
    meta = jnp.concatenate([routes.astype(F32).T, gates.T], axis=0)
    rnat = routes.astype(F32).reshape(1, SLOT)
    hidden, weight = run_main(
        cotangent, meta, rnat, pre_act, down_weight.reshape(2, 2, 4, 4, 16, D)
    )
    return run_grad(hidden, pre_act), weight[None]


def solution(mesh):
    in_specs = (
        P(("grp", "ep"), None),
        P(("grp", "ep"), None),
        P(("grp", "ep"), None),
        P(("grp", "ep"), None, None),
        P("ep", None, None),
    )
    out_specs = (P(("grp", "ep"), None, None), P("ep", "grp", None))
    return jax.shard_map(local, mesh=mesh, in_specs=in_specs, out_specs=out_specs, check_vma=False)
```

```python
import functools

import jax
import jax.numpy as jnp
from jax import lax
from jax.experimental import pallas as pl
from jax.experimental.pallas import tpu as pltpu
from jax.sharding import PartitionSpec as P

MESH = pl.DeviceIdType.MESH
BF = jnp.bfloat16
F32 = jnp.float32

TOK = 128
TOPK = 4
SLOT = TOK * TOPK
HID = 1024
D = 3584
CAP = 20
NX, NZ = 4, 4
NJ = 8
NQ = 4
DQ = D // NQ
ROW = NX * CAP
COLD = NJ * ROW
HALF = D // 2
HALFHID = HID // 2


def dot(a, b, dims=((1,), (0,))):
    return lax.dot_general(a, b, (dims, ((), ())), preferred_element_type=F32)


NN = ((1,), (0,))
NT = ((1,), (1,))
TN = ((0,), (0,))


def iota(shape, dim):
    return lax.broadcasted_iota(jnp.int32, shape, dim)


def onehot(flag):
    return flag.astype(F32).astype(BF)


def main_kernel(
    cot, rt, gt, pre, w,
    hid, wg,
    meta, cg, ch, mg, pa, wq,
    ohx, sel, ohg, pm, px, gc,
    acts, actx, actp, actr, actb,
    s, sr, sp, hacc, hgx, ret,
    wgs, cr, yr,
    a1r, a2s, a2r, a3s, a3r, ags, wh,
    ahot, aht, at, hht, hhs, hp, rsb, gp, g1, g2, g3,
    ssem, rsem, lsem,
):
    g, e = lax.axis_index("grp"), lax.axis_index("ep")
    yl, c = g // 2, g % 2
    x, yh, z = e // 8, (e // 4) % 2, e % 4
    us, vs = (x, z), (z, x)

    def dev(dx=0, dyh=0, dz=0, dyl=0, dc=0):
        return (
            ((yl + dyl) % 2) * 2 + (c + dc) % 2,
            (((x + dx) % 4) * 2 + (yh + dyh) % 2) * 4 + (z + dz) % 4,
        )

    def way(p, du=0, dv=0, **to):
        return dict(dx=(du, dv)[p], dz=(dv, du)[p], **to)

    counts = [0, 0]

    def remote(src, dst, **to):
        k = counts[0]
        counts[0] += 1
        cp = pltpu.make_async_remote_copy(
            src_ref=src, dst_ref=dst, send_sem=ssem.at[k], recv_sem=rsem.at[k],
            device_id=dev(**to), device_id_type=MESH,
        )
        cp.start()
        return cp

    def here(src, dst):
        k = counts[1]
        counts[1] += 1
        cp = pltpu.make_async_copy(src, dst, lsem.at[k])
        cp.start()
        return cp

    sent = []

    def arrived(copies):
        for cp in copies:
            cp.wait_recv()
        sent.extend(copies)

    def left(copies):
        gone = [id(cp) for cp in copies]
        sent[:] = [cp for cp in sent if id(cp) not in gone]
        for cp in copies:
            cp.wait_send()

    def cols(q):
        return pl.ds(q * DQ, DQ)

    def half(p):
        return pl.ds(p * HALF, HALF)

    def hh(p):
        return pl.ds(p * HALFHID, HALFHID)

    peers = set()
    for p in range(2):
        for d in range(4):
            for a in range(2):
                for b in range(2):
                    peers.add(tuple(sorted(way(p, dv=d, dyh=a, dyl=b, dc=0).items())))
            for cc in range(2):
                peers.add(tuple(sorted(way(p, du=d, dyh=0, dyl=0, dc=cc).items())))
    peers = [dict(t) for t in sorted(peers) if any(v for _, v in t)]
    barrier = pltpu.get_barrier_semaphore()
    for to in peers:
        pl.semaphore_signal(barrier, inc=1, device_id=dev(**to), device_id_type=MESH)
    ORDER = (0, 2, 1, 3)
    own_cot = {}
    for q in ORDER:
        own_cot[q] = here(cot.at[:, cols(q)], cg.at[q, pl.ds(us[q // 2] * TOK, TOK)])
    NP = 4
    pt = TOK // NP
    pa_copy = [here(pre.at[pl.ds(i * pt, pt)], pa.at[i]) for i in range(2)]
    meta[0:TOPK, :] = rt[...].astype(F32)
    meta[TOPK:2 * TOPK, :] = gt[...]
    pl.semaphore_wait(barrier, len(peers))

    cot_cp = {}

    def send_cot(q):
        p = q // 2
        cot_cp[q] = [
            remote(cot.at[:, cols(q)], cg.at[q, pl.ds(us[p] * TOK, TOK)], **way(p, du=d))
            for d in (1, 3)
        ]

    fwd_cp = {}

    def pass_on(q):
        p = q // 2
        arrived(cot_cp[q])
        fwd_cp[q] = []
        for d, k in ((1, 0), (3, TOK // 2)):
            r = pl.ds(((us[p] - d + 4) % 4) * TOK + k, TOK // 2)
            fwd_cp[q].append(remote(cg.at[q, r], cg.at[q, r], **way(p, du=d)))

    meta_cp = []
    for p in range(2):
        for cc in range(2):
            for d in range(4):
                if cc or d:
                    meta_cp.append(remote(meta, mg.at[p, cc * 4 + us[p]], **way(p, du=d, dc=cc)))
    send_cot(0)
    send_cot(2)
    for p in range(2):
        mg[p, us[p]] = meta[...]

    rn = jnp.zeros((8, SLOT), F32)
    for k in range(TOPK):
        rn = rn + dot(
            jnp.broadcast_to(meta[k:k + 1], (8, TOK)).astype(BF),
            onehot(iota((TOK, SLOT), 1) == iota((TOK, SLOT), 0) * TOPK + k),
        )
    rn = rn[0:1]
    ei = iota((32, SLOT), 0)
    eid = ei.astype(F32)
    member = (rn == eid).astype(F32)
    tri = onehot(iota((SLOT, SLOT), 0) < iota((SLOT, SLOT), 1))
    rank = dot(member.astype(BF), tri)
    hotv = (jnp.sum(member, axis=1, keepdims=True) >= 64.0).astype(F32)
    token = lax.shift_right_logical(iota((32, SLOT), 1), 2).astype(F32)
    turned = ((ei & 3) * 8 + (ei & 4) + lax.shift_right_logical(ei, 3)).astype(F32)
    cold = member * (1.0 - hotv)
    for p in range(2):
        order = (eid, turned)[p]
        key = jnp.sum(cold * (order * CAP + rank) - (member - cold), axis=0, keepdims=True)
        for i in range(COLD // 128):
            ohx[p, pl.ds(i * 128, 128), :] = onehot(
                iota((128, SLOT), 0).astype(F32) + i * 128.0 == key
            )
    key = jnp.sum(member * hotv * (token + 1.0), axis=0, keepdims=True) - 1.0
    sel[...] = onehot(iota((128, SLOT), 0).astype(F32) == key)
    e1 = iota((32, 1), 0)

    def hot_is(flag):
        return jnp.sum(hotv * flag.astype(F32), axis=0, keepdims=True)

    hotid = jnp.sum(hotv * e1.astype(F32), axis=0, keepdims=True)
    hot_x = [hot_is(lax.shift_right_logical(e1, 3) == k) for k in range(4)]
    hot_z = [hot_is((e1 & 3) == k) for k in range(4)]
    hot_y = [hot_is((lax.shift_right_logical(e1, 2) & 1) == k) for k in range(2)]
    hot_u, hot_v = (hot_x, hot_z), (hot_z, hot_x)

    pass_on(0)
    pass_on(2)
    send_cot(1)
    send_cot(3)
    w_copy = {q: here(w.at[:, :, :, :, :, cols(q)], wq.at[q]) for q in ORDER}

    arrived(meta_cp)
    tri1 = onehot(iota((TOK, TOK), 0) < iota((TOK, TOK), 1))
    i8 = iota((NJ, TOK), 0)
    rows80 = iota((ROW, SLOT), 0).astype(F32)
    for p in range(2):
        if p == 0:
            ej = (i8 + 8 * x).astype(F32)
        else:
            ej = ((i8 & 3) * 8 + (i8 & 4) + z).astype(F32)
        keys, gates8 = [], []
        for b in range(NX):
            m = mg[p, b]
            hit = [(m[k:k + 1] == ej) for k in range(TOPK)]
            mem8 = sum(f.astype(F32) for f in hit)
            gates8.append(sum(jnp.where(hit[k], m[4 + k:5 + k], 0.0) for k in range(TOPK)))
            rank8 = dot(mem8.astype(BF), tri1)
            mem8 = mem8 * (ej != hotid).astype(F32)
            keys.append(jnp.where(mem8 > 0, rank8 + CAP * b, -1.0))
        keys = jnp.concatenate(keys, axis=1)
        gates8 = jnp.concatenate(gates8, axis=1)
        for j in range(NJ):
            flag = rows80 == keys[j:j + 1]
            ohg[p, pl.ds(j * ROW, ROW), :] = onehot(flag)
            col = jnp.sum(jnp.where(flag, gates8[j:j + 1], 0.0), axis=1, keepdims=True)
            gc[p, pl.ds(j * ROW, ROW), :] = jnp.broadcast_to(col, (ROW, 128))

    def spread(p, src, dst):
        v = vs[p]
        cps = [
            remote(
                src.at[pl.ds((((yh + a) % 2) * 4 + (v + d) % 4) * ROW, ROW)],
                dst.at[pl.ds((yh * 4 + v) * ROW, ROW)], **way(p, dv=d, dyh=a, dyl=a),
            )
            for a, d in ((0, 1), (0, 3), (1, 0), (0, 2), (1, 1), (1, 3), (1, 2))
        ]
        own = pl.ds((yh * 4 + v) * ROW, ROW)
        return cps, here(src.at[own], dst.at[own])

    sr_cp, ch_cp = {}, {}

    def piece(q):
        p = q // 2
        own_cot[q].wait()
        arrived(fwd_cp[q])

        def step(i, carry):
            r = pl.ds(pl.multiple_of(i * 320, 320), 320)
            s[q, r, :] = (dot(ohg[p, r, :], cg[q]) * gc[p, r, 0:1]).astype(BF)
            return carry

        lax.fori_loop(0, 2, step, 0)
        sr_cp[q] = spread(p, s.at[q], sr.at[q])
        ch_cp[q] = remote(cg.at[q], ch.at[q], dc=1)

    piece(0)
    piece(2)
    a1_cp, a1_own = [], []
    for p in range(2):
        a1_cp.append([
            remote(w.at[yl, c, :, (vs[p] + d) % 4, :, half(p)], a1r.at[p, vs[p]], **way(p, dv=d))
            for d in (1, 3, 2)
        ])
        a1_own.append(here(w.at[yl, c, :, vs[p], :, half(p)], a1r.at[p, vs[p]]))
    pass_on(1)
    pass_on(3)
    for i in range(NP):
        pa_copy[i].wait()

        def act_step(j, carry):
            rows = pa[i % 2, pl.ds(j * 8, 8)].reshape(32, 2 * HID).astype(F32)
            gate, up = rows[:, :HID], rows[:, HID:]
            hid[pl.ds(pl.multiple_of(i * pt * 4 + j * 32, 32), 32), :] = (
                gate * jax.nn.sigmoid(gate) * up
            ).astype(BF)
            return carry

        lax.fori_loop(0, pt // 8, act_step, 0)
        if i + 2 < NP:
            pa_copy.append(here(pre.at[pl.ds((i + 2) * pt, pt)], pa.at[i % 2]))

    actx_cp, actx_own = [], []
    for p in range(2):

        def acts_step(i, carry):
            r = pl.ds(pl.multiple_of(i * 320, 320), 320)
            acts[p, r, :] = dot(ohx[p, r, :], hid[:, hh(p)]).astype(BF)
            return carry

        lax.fori_loop(0, 2, acts_step, 0)
    ahot[...] = dot(sel[...], hid[...]).astype(BF)
    eye = onehot(iota((TOK, TOK), 0) == iota((TOK, TOK), 1))
    aht[...] = dot(ahot[...], eye, TN).astype(BF).reshape(2, HID // 2, TOK)

    def ring_part(p, d, cc):
        return pl.ds(256 * ((c + cc) % 2) + 64 * ((us[p] + d) % 4), 64)

    for p in range(2):
        u = us[p]
        actx_cp.append([
            remote(acts.at[p, pl.ds(((u + d) % 4) * 160, 160)], actx.at[p, pl.ds(u * 160, 160)],
                   **way(p, du=d))
            for d in (1, 3, 2)
        ])
        actx_own.append(here(acts.at[p, pl.ds(u * 160, 160)], actx.at[p, pl.ds(u * 160, 160)]))
    at_cp, at_own = [], []
    for p in range(2):
        at_cp.append([])
        for cc in range(2):
            for d in range(4):
                src = aht.at[:, ring_part(p, d, cc), :]
                dst = at.at[p, :, :, pl.ds((cc * 4 + us[p]) * TOK, TOK)]
                if cc or d:
                    at_cp[p].append(remote(src, dst, **way(p, du=d, dc=cc)))
                else:
                    at_own.append(here(src, dst))

    o = iota((COLD, 128), 0)
    oj = sum((o >= ROW * k).astype(jnp.int32) for k in range(1, NJ))
    orem = o - ROW * oj
    ob = sum((orem >= CAP * k).astype(jnp.int32) for k in range(1, NX))
    want = ob * 160 + oj * CAP + (orem - CAP * ob)
    for k in range(COLD // 128):
        pm[:, pl.ds(k * 128, 128)] = onehot(want == iota((COLD, 128), 1) + k * 128)
    o = iota((4 * ROW, 4 * ROW), 0)
    oj = sum((o >= ROW * k).astype(jnp.int32) for k in range(1, 4))
    orem = o - ROW * oj
    ob = sum((orem >= CAP * k).astype(jnp.int32) for k in range(1, NX))
    px[...] = onehot(ob * ROW + oj * CAP + (orem - CAP * ob) == iota((4 * ROW, 4 * ROW), 1))

    def turn(src, dst):
        for k in range(2):
            r = pl.ds(k * 4 * ROW, 4 * ROW)
            dst[r, :] = dot(px[...], src[r, :]).astype(BF)

    yr_cp = {}

    def expert_hidden(n):
        q = ORDER[n]
        w_copy[q].wait()
        sr_cp[q][1].wait()
        arrived(sr_cp[q][0])
        rows = sr.at[q]
        if q >= 2:
            turn(sr.at[q], sp)
            rows = sp
        for h in range(2):
            for k in range(2):
                r = pl.ds(512 * h + 256 * k, 256)
                part = dot(rows[...], wq[q, h, k].reshape(256, DQ), NT)
                hacc[:, r] = part if n == 0 else hacc[:, r] + part

    def expert_weight(n):
        q = ORDER[n]
        rows = sp if q >= 2 else sr.at[q]
        for p in range(2):
            act = (actr.at[0], actb)[p]

            def wg_step(i, carry):
                r = pl.ds(pl.multiple_of(i * 256, 256), 256)
                wgs[pl.ds(pl.multiple_of(p * HALFHID + i * 256, 256), 256), :] = dot(
                    act[:, r], rows[...], TN
                ).astype(BF)
                return carry

            lax.fori_loop(0, 2, wg_step, 0)
        cr_cp = [
            remote(wgs.at[pl.ds(512 * h + 256 * ((c + 1) % 2), 256)], cr.at[n % 2, h], dc=1)
            for h in range(2)
        ]

        for cp in cr_cp:
            cp.wait()
        there, stay = (yl + 1) % 2, yl
        left(sr_cp[q][0])
        s[q, 0:256, :] = (
            wgs[pl.ds(512 * there + 256 * c, 256), :].astype(F32)
            + cr[n % 2, there].astype(F32)
        ).astype(BF)
        yr_cp[q] = remote(s.at[q, pl.ds(0, 256)], yr.at[q], dyl=1)
        wg[:, cols(q)] = (
            wgs[pl.ds(512 * stay + 256 * c, 256), :].astype(F32)
            + cr[n % 2, stay].astype(F32)
        ).astype(BF)

    a2_cp, a2_own, a3_cp, wh_cp, wh_own = [], [], [], [], []
    for p in range(2):
        a1_own[p].wait()
        arrived(a1_cp[p])
        for k in range(4):
            a2s[p, k] = sum(a1r[p, i, k].astype(F32) * hot_v[p][i] for i in range(4)).astype(BF)
        u = us[p]
        a2_cp.append([
            remote(a2s.at[p, (u + d) % 4], a2r.at[p, u], **way(p, du=d)) for d in (1, 3, 2)
        ])
        a2_own.append(here(a2s.at[p, u], a2r.at[p, u]))
    for p in range(2):
        a2_own[p].wait()
        arrived(a2_cp[p])
        a3s[p] = sum(a2r[p, k].astype(F32) * hot_u[p][k] for k in range(4)).astype(BF)
        a3_cp.append(remote(a3s.at[p], a3r.at[p], dyh=1))
    actr_cp, actr_own = [], []
    for p in range(2):
        actx_own[p].wait()
        arrived(actx_cp[p])

        def actp_step(i, carry):
            r = pl.ds(pl.multiple_of(i * 320, 320), 320)
            actp[p, r, :] = dot(pm[r, :], actx[p]).astype(BF)
            return carry

        lax.fori_loop(0, 2, actp_step, 0)
        a, b = spread(p, actp.at[p], actr.at[p])
        actr_cp.append(a)
        actr_own.append(b)

    mine = hot_y[0] * (yh == 0).astype(F32) + hot_y[1] * (yh == 1).astype(F32)
    for p in range(2):
        arrived([a3_cp[p]])
        ags[p] = (
            a3s[p].astype(F32) * mine + a3r[p].astype(F32) * (1.0 - mine)
        ).astype(BF)
        slot = wh.at[p, yl, vs[p]]
        wh_cp.append([
            remote(ags.at[p], slot, **way(p, dv=d, dyl=b))
            for b in range(2) for d in range(4) if b or d
        ])
        wh_own.append(here(ags.at[p], slot))

    piece(1)
    piece(3)
    sh = wgs
    diag = iota((TOK, TOK), 0) == iota((TOK, TOK), 1)
    hh_cp, hh_own, rs_cp, rs_own = [], [], [], []
    for p in range(2):
        at_own[p].wait()
        arrived(at_cp[p])
        wh_own[p].wait()
        arrived(wh_cp[p])
        for i in range(2):
            q = 2 * p + i
            arrived([ch_cp[q]])
            for b in range(2 * NX):
                m = mg[p, b]
                row = sum(
                    jnp.where(m[k:k + 1] == hotid, m[4 + k:5 + k], 0.0) for k in range(TOPK)
                )
                col = jnp.sum(jnp.where(diag, row, 0.0), axis=1, keepdims=True)
                block = (cg, ch)[b // NX][q, pl.ds((b % NX) * TOK, TOK), :]
                sh[pl.ds(b * TOK, TOK), :] = (block.astype(F32) * col).astype(BF)
            hp[q] = dot(at[p].reshape(128, 8 * TOK), sh[...]).astype(BF)
            part = dot(wh[p, :, :, :, pl.ds(i * DQ, DQ)].reshape(128, DQ), sh[...], NT)
            for k in range(8):
                t, r = pl.ds(k * 128, 128), pl.ds((k % 4) * 128, 128)
                if i == 0:
                    gc[k // 4, r, :] = part[:, k * 128:(k + 1) * 128]
                else:
                    hhs[p, :, :, t] = (
                        gc[k // 4, r, :] + part[:, k * 128:(k + 1) * 128]
                    ).astype(BF).reshape(2, 64, TOK)
        hh_cp.append([])
        for cc in range(2):
            for d in range(4):
                src = hhs.at[p, :, :, pl.ds((cc * 4 + (us[p] + d) % 4) * TOK, TOK)]
                dst = hht.at[p, :, pl.ds(256 * c + 64 * us[p], 64), :]
                if cc or d:
                    hh_cp[p].append(remote(src, dst, **way(p, du=d, dc=cc)))
                else:
                    hh_own.append(here(src, dst))
        rs_cp.append([])
        k = 1
        for a in range(2):
            for b in range(2):
                for d in range(4):
                    src = hp.at[
                        2 * p + (yh + a) % 2,
                        pl.ds(((yl + b) % 2) * 64 + ((vs[p] + d) % 4) * 16, 16),
                    ]
                    if a or b or d:
                        rs_cp[p].append(
                            remote(src, rsb.at[p, k], **way(p, dv=d, dyh=a, dyl=b))
                        )
                        k += 1
                    else:
                        rs_own.append(here(src, rsb.at[p, 0]))

    for p in range(2):
        actr_own[p].wait()
        arrived(actr_cp[p])
    turn(actr.at[1], actb)
    for n in range(2):
        expert_hidden(n)
        expert_weight(n)

    expert_hidden(2)
    expert_hidden(3)
    for p in range(2):
        left(actx_cp[p])
    hg = acts
    hgx_cp, hgx_own = [], []
    for p in range(2):
        if p == 0:
            hg[0] = hacc[:, hh(0)].astype(BF)
        else:
            for k in range(2):
                r = pl.ds(k * 4 * ROW, 4 * ROW)
                hg[1, r, :] = dot(px[...], hacc[r, hh(1)].astype(BF)).astype(BF)
        a, b = spread(p, hg.at[p], hgx.at[p])
        hgx_cp.append(a)
        hgx_own.append(b)

    g1_cp, g1_own, g2_cp, g2_own, g3_cp, g3_own = [], [], [], [], [], []
    for p in range(2):
        rs_own[p].wait()
        arrived(rs_cp[p])
        gp[p] = sum(rsb[p, k].astype(F32) for k in range(16)).astype(BF)
        g1_cp.append([remote(gp.at[p], g1.at[p, vs[p]], **way(p, dv=d)) for d in (1, 3, 2)])
        g1_own.append(here(gp.at[p], g1.at[p, vs[p]]))

    for p in range(2):
        g1_own[p].wait()
        arrived(g1_cp[p])
        g2_cp.append(remote(g1.at[p], g2.at[p, yh], dyh=1))
        g2_own.append(here(g1.at[p], g2.at[p, yh]))
    expert_weight(2)
    for p in range(2):
        g2_own[p].wait()
        arrived([g2_cp[p]])
        g3_cp.append([remote(g2.at[p], g3.at[p, us[p]], **way(p, du=d)) for d in (1, 3, 2)])
        g3_own.append(here(g2.at[p], g3.at[p, us[p]]))
    expert_weight(3)

    hgp = actp
    ret_cp, ret_own = [], []
    for p in range(2):
        left(actr_cp[p])
        hgx_own[p].wait()
        arrived(hgx_cp[p])
        for i in range(5):
            r = pl.ds(i * 128, 128)
            hgp[p, r, :] = dot(pm[:, r], hgx[p], TN).astype(BF)
        u = us[p]
        ret_cp.append([
            remote(hgp.at[p, pl.ds(((u + d) % 4) * 160, 160)], ret.at[p, pl.ds(u * 160, 160)],
                   **way(p, du=d))
            for d in (1, 3, 2)
        ])
        ret_own.append(here(hgp.at[p, pl.ds(u * 160, 160)], ret.at[p, pl.ds(u * 160, 160)]))

    for p in range(2):
        hh_own[p].wait()
        arrived(hh_cp[p])
    ahot[...] = (
        dot(eye, hht[0].reshape(HID, TOK), NT) + dot(eye, hht[1].reshape(HID, TOK), NT)
    ).astype(BF)

    for n, q in enumerate(ORDER):
        yr_cp[q].wait_recv()
        sent.append(yr_cp[q])
        wg[:, cols(q)] = (wg[:, cols(q)].astype(F32) + yr[q].astype(F32)).astype(BF)
    for p in range(2):
        ret_own[p].wait()
        arrived(ret_cp[p])
        for i in range(2):
            r, t = pl.ds(i * 256, 256), pl.ds(p * HALFHID + i * 256, 256)
            hid[:, t] = (dot(ohx[p], ret[p, :, r], TN) + dot(sel[...], ahot[:, t], TN)).astype(BF)

    own = (e1 == e).astype(F32)
    is_hot = jnp.sum(own * hotv, axis=0, keepdims=True)
    for p in range(2):
        g3_own[p].wait()
        arrived(g3_cp[p])
        for ut in range(4):
            for i in range(2):
                for vt in range(4):
                    r, k = pl.ds(64 * ut + 16 * vt, 16), cols(2 * p + i)
                    wg[r, k] = (
                        wg[r, k].astype(F32) * (1.0 - is_hot)
                        + g3[p, ut, i, vt].astype(F32) * is_hot
                    ).astype(BF)
    for cp in sent:
        cp.wait_send()


def vm(*shape, dtype=BF):
    return pltpu.VMEM(shape, dtype)


def run_main(cot, rt, gt, pre, w):
    anyw = pl.BlockSpec(memory_space=pl.ANY)
    vmem = pl.BlockSpec(memory_space=pltpu.VMEM)
    scratch = [
        vm(8, 128, dtype=F32),
        vm(NQ, SLOT, DQ), vm(NQ, SLOT, DQ), vm(2, 8, 8, 128, dtype=F32),
        vm(2, TOK // 4, TOPK, 2 * HID), vm(NQ, 2, 2, 4, 4, 16, DQ),
        vm(2, COLD, SLOT), vm(TOK, SLOT), vm(2, COLD, SLOT), vm(COLD, COLD),
        vm(4 * ROW, 4 * ROW), vm(2, COLD, 128, dtype=F32),
        vm(2, COLD, HALFHID), vm(2, COLD, HALFHID), vm(2, COLD, HALFHID), vm(2, COLD, HALFHID),
        vm(COLD, HALFHID),
        vm(NQ, COLD, DQ), vm(NQ, COLD, DQ), vm(COLD, DQ), vm(COLD, HID, dtype=F32),
        vm(2, COLD, HALFHID), vm(2, COLD, HALFHID),
        vm(HID, DQ), vm(2, 2, 256, DQ), vm(NQ, 256, DQ),
        vm(2, 4, 4, 16, HALF), vm(2, 4, 16, HALF), vm(2, 4, 16, HALF),
        vm(2, 16, HALF), vm(2, 16, HALF), vm(2, 16, HALF), vm(2, 2, 4, 16, HALF),
        vm(TOK, HID), vm(2, HID // 2, TOK), vm(2, 2, 64, 8 * TOK), vm(2, 2, HID // 2, TOK),
        vm(2, 2, 64, 8 * TOK), vm(NQ, 128, DQ),
        vm(2, 16, 16, DQ), vm(2, 16, DQ), vm(2, 4, 16, DQ), vm(2, 2, 4, 16, DQ),
        vm(2, 4, 2, 4, 16, DQ),
        pltpu.SemaphoreType.DMA((256,)), pltpu.SemaphoreType.DMA((256,)),
        pltpu.SemaphoreType.DMA((64,)),
    ]
    return pl.pallas_call(
        main_kernel,
        out_shape=(
            jax.ShapeDtypeStruct((SLOT, HID), BF),
            jax.ShapeDtypeStruct((256, D), BF),
        ),
        in_specs=[anyw, vmem, vmem, anyw, anyw],
        out_specs=(vmem, vmem),
        scratch_shapes=scratch,
        compiler_params=pltpu.CompilerParams(
            collective_id=0, has_side_effects=True, vmem_limit_bytes=61 * 1024 * 1024
        ),
        cost_estimate=pl.CostEstimate(
            flops=22 * 10**9, bytes_accessed=16 * 10**6, transcendentals=10**6
        ),
    )(cot, rt, gt, pre, w)


def grad_kernel(h, p, o):
    n = h.shape[0]
    back = h[...].astype(F32)
    rows = p[...].reshape(n, 2 * HID).astype(F32)
    gate, up = rows[:, :HID], rows[:, HID:]
    sig = jax.nn.sigmoid(gate)
    left = back * up * sig * (1.0 + gate * (1.0 - sig))
    right = back * gate * sig
    o[:, :, :HID] = left.astype(BF).reshape(n // TOPK, TOPK, HID)
    o[:, :, HID:] = right.astype(BF).reshape(n // TOPK, TOPK, HID)


def run_grad(hidden, pre):
    n = 16
    return pl.pallas_call(
        grad_kernel,
        grid=(TOK // n,),
        out_shape=jax.ShapeDtypeStruct((TOK, TOPK, 2 * HID), BF),
        in_specs=[
            pl.BlockSpec((n * TOPK, HID), lambda i: (i, 0)),
            pl.BlockSpec((n, TOPK, 2 * HID), lambda i: (i, 0, 0)),
        ],
        out_specs=pl.BlockSpec((n, TOPK, 2 * HID), lambda i: (i, 0, 0)),
        compiler_params=pltpu.CompilerParams(vmem_limit_bytes=24 * 1024 * 1024),
    )(hidden, pre)


def local(cotangent, routes, gates, pre_act, down_weight):
    hidden, weight = run_main(
        cotangent, routes.T, gates.T, pre_act, down_weight.reshape(2, 2, 4, 4, 16, D)
    )
    return run_grad(hidden, pre_act), weight[None]


def solution(mesh):
    in_specs = (
        P(("grp", "ep"), None),
        P(("grp", "ep"), None),
        P(("grp", "ep"), None),
        P(("grp", "ep"), None, None),
        P("ep", None, None),
    )
    out_specs = (P(("grp", "ep"), None, None), P("ep", "grp", None))
    return jax.shard_map(local, mesh=mesh, in_specs=in_specs, out_specs=out_specs, check_vma=False)
```

```python
import functools

import jax
import jax.numpy as jnp
from jax import lax
from jax.experimental import pallas as pl
from jax.experimental.pallas import tpu as pltpu
from jax.sharding import PartitionSpec as P

MESH = pl.DeviceIdType.MESH
BF = jnp.bfloat16
F32 = jnp.float32

TOK = 128
TOPK = 4
SLOT = TOK * TOPK
HID = 1024
D = 3584
CAP = 20
NX, NZ = 4, 4
NJ = 8
NQ = 4
DQ = D // NQ
ROW = NX * CAP
COLD = NJ * ROW
HALF = D // 2
HALFHID = HID // 2


def dot(a, b, dims=((1,), (0,))):
    return lax.dot_general(a, b, (dims, ((), ())), preferred_element_type=F32)


NN = ((1,), (0,))
NT = ((1,), (1,))
TN = ((0,), (0,))


def iota(shape, dim):
    return lax.broadcasted_iota(jnp.int32, shape, dim)


def onehot(flag):
    return flag.astype(F32).astype(BF)


def main_kernel(
    cot, rt, gt, pre, w,
    hid, wg,
    meta, cg, ch, mg, pa, wq,
    ohx, sel, ohg, pm, px, gc,
    acts, actx, actp, actr, actb,
    s, sr, sp, hacc, hgx, ret,
    wgs, cr, yr,
    a1r, a2s, a2r, a3s, a3r, ags, wh,
    ahot, aht, at, hht, hhs, hp, rsb, gp, g1, g2, g3,
    ssem, rsem, lsem,
):
    g, e = lax.axis_index("grp"), lax.axis_index("ep")
    yl, c = g // 2, g % 2
    x, yh, z = e // 8, (e // 4) % 2, e % 4
    us, vs = (x, z), (z, x)

    def dev(dx=0, dyh=0, dz=0, dyl=0, dc=0):
        return (
            ((yl + dyl) % 2) * 2 + (c + dc) % 2,
            (((x + dx) % 4) * 2 + (yh + dyh) % 2) * 4 + (z + dz) % 4,
        )

    def way(p, du=0, dv=0, **to):
        return dict(dx=(du, dv)[p], dz=(dv, du)[p], **to)

    counts = [0, 0]

    def remote(src, dst, **to):
        k = counts[0]
        counts[0] += 1
        cp = pltpu.make_async_remote_copy(
            src_ref=src, dst_ref=dst, send_sem=ssem.at[k], recv_sem=rsem.at[k],
            device_id=dev(**to), device_id_type=MESH,
        )
        cp.start()
        return cp

    def here(src, dst):
        k = counts[1]
        counts[1] += 1
        cp = pltpu.make_async_copy(src, dst, lsem.at[k])
        cp.start()
        return cp

    sent = []

    def arrived(copies):
        for cp in copies:
            cp.wait_recv()
        sent.extend(copies)

    def left(copies):
        gone = [id(cp) for cp in copies]
        sent[:] = [cp for cp in sent if id(cp) not in gone]
        for cp in copies:
            cp.wait_send()

    def cols(q):
        return pl.ds(q * DQ, DQ)

    def half(p):
        return pl.ds(p * HALF, HALF)

    def hh(p):
        return pl.ds(p * HALFHID, HALFHID)

    peers = set()
    for p in range(2):
        for d in range(4):
            for a in range(2):
                for b in range(2):
                    peers.add(tuple(sorted(way(p, dv=d, dyh=a, dyl=b, dc=0).items())))
            for cc in range(2):
                peers.add(tuple(sorted(way(p, du=d, dyh=0, dyl=0, dc=cc).items())))
    peers = [dict(t) for t in sorted(peers) if any(v for _, v in t)]
    barrier = pltpu.get_barrier_semaphore()
    for to in peers:
        pl.semaphore_signal(barrier, inc=1, device_id=dev(**to), device_id_type=MESH)
    ORDER = (0, 2, 1, 3)
    own_cot = {}
    for q in ORDER:
        own_cot[q] = here(cot.at[:, cols(q)], cg.at[q, pl.ds(us[q // 2] * TOK, TOK)])
    NP = 4
    pt = TOK // NP
    pa_copy = [here(pre.at[pl.ds(i * pt, pt)], pa.at[i]) for i in range(2)]
    meta[0:TOPK, :] = rt[...].astype(F32)
    meta[TOPK:2 * TOPK, :] = gt[...]
    pl.semaphore_wait(barrier, len(peers))

    cot_cp = {}

    def send_cot(q):
        p = q // 2
        cot_cp[q] = [
            remote(cot.at[:, cols(q)], cg.at[q, pl.ds(us[p] * TOK, TOK)], **way(p, du=d))
            for d in (1, 3)
        ]

    fwd_cp = {}

    def pass_on(q):
        p = q // 2
        arrived(cot_cp[q])
        fwd_cp[q] = []
        for d, k in ((1, 0), (3, TOK // 2)):
            r = pl.ds(((us[p] - d + 4) % 4) * TOK + k, TOK // 2)
            fwd_cp[q].append(remote(cg.at[q, r], cg.at[q, r], **way(p, du=d)))

    meta_cp = []
    for p in range(2):
        for cc in range(2):
            for d in range(4):
                if cc or d:
                    meta_cp.append(remote(meta, mg.at[p, cc * 4 + us[p]], **way(p, du=d, dc=cc)))
    send_cot(0)
    send_cot(2)
    for p in range(2):
        mg[p, us[p]] = meta[...]

    rn = jnp.zeros((8, SLOT), F32)
    for k in range(TOPK):
        rn = rn + dot(
            jnp.broadcast_to(meta[k:k + 1], (8, TOK)).astype(BF),
            onehot(iota((TOK, SLOT), 1) == iota((TOK, SLOT), 0) * TOPK + k),
        )
    rn = rn[0:1]
    ei = iota((32, SLOT), 0)
    eid = ei.astype(F32)
    member = (rn == eid).astype(F32)
    tri = onehot(iota((SLOT, SLOT), 0) < iota((SLOT, SLOT), 1))
    rank = dot(member.astype(BF), tri)
    hotv = (jnp.sum(member, axis=1, keepdims=True) >= 64.0).astype(F32)
    token = lax.shift_right_logical(iota((32, SLOT), 1), 2).astype(F32)
    turned = ((ei & 3) * 8 + (ei & 4) + lax.shift_right_logical(ei, 3)).astype(F32)
    cold = member * (1.0 - hotv)
    for p in range(2):
        order = (eid, turned)[p]
        key = jnp.sum(cold * (order * CAP + rank) - (member - cold), axis=0, keepdims=True)
        for i in range(COLD // 128):
            ohx[p, pl.ds(i * 128, 128), :] = onehot(
                iota((128, SLOT), 0).astype(F32) + i * 128.0 == key
            )
    key = jnp.sum(member * hotv * (token + 1.0), axis=0, keepdims=True) - 1.0
    sel[...] = onehot(iota((128, SLOT), 0).astype(F32) == key)
    e1 = iota((32, 1), 0)

    def hot_is(flag):
        return jnp.sum(hotv * flag.astype(F32), axis=0, keepdims=True)

    hotid = jnp.sum(hotv * e1.astype(F32), axis=0, keepdims=True)
    hot_x = [hot_is(lax.shift_right_logical(e1, 3) == k) for k in range(4)]
    hot_z = [hot_is((e1 & 3) == k) for k in range(4)]
    hot_y = [hot_is((lax.shift_right_logical(e1, 2) & 1) == k) for k in range(2)]
    hot_u, hot_v = (hot_x, hot_z), (hot_z, hot_x)

    pass_on(0)
    pass_on(2)
    send_cot(1)
    send_cot(3)
    w_copy = {q: here(w.at[:, :, :, :, :, cols(q)], wq.at[q]) for q in ORDER}

    arrived(meta_cp)
    tri1 = onehot(iota((TOK, TOK), 0) < iota((TOK, TOK), 1))
    i8 = iota((NJ, TOK), 0)
    rows80 = iota((ROW, SLOT), 0).astype(F32)
    for p in range(2):
        if p == 0:
            ej = (i8 + 8 * x).astype(F32)
        else:
            ej = ((i8 & 3) * 8 + (i8 & 4) + z).astype(F32)
        keys, gates8 = [], []
        for b in range(NX):
            m = mg[p, b]
            hit = [(m[k:k + 1] == ej) for k in range(TOPK)]
            mem8 = sum(f.astype(F32) for f in hit)
            gates8.append(sum(jnp.where(hit[k], m[4 + k:5 + k], 0.0) for k in range(TOPK)))
            rank8 = dot(mem8.astype(BF), tri1)
            mem8 = mem8 * (ej != hotid).astype(F32)
            keys.append(jnp.where(mem8 > 0, rank8 + CAP * b, -1.0))
        keys = jnp.concatenate(keys, axis=1)
        gates8 = jnp.concatenate(gates8, axis=1)
        for j in range(NJ):
            flag = rows80 == keys[j:j + 1]
            ohg[p, pl.ds(j * ROW, ROW), :] = onehot(flag)
            col = jnp.sum(jnp.where(flag, gates8[j:j + 1], 0.0), axis=1, keepdims=True)
            gc[p, pl.ds(j * ROW, ROW), :] = jnp.broadcast_to(col, (ROW, 128))

    def spread(p, src, dst):
        v = vs[p]
        cps = [
            remote(
                src.at[pl.ds((((yh + a) % 2) * 4 + (v + d) % 4) * ROW, ROW)],
                dst.at[pl.ds((yh * 4 + v) * ROW, ROW)], **way(p, dv=d, dyh=a, dyl=a),
            )
            for a, d in ((0, 1), (0, 3), (1, 0), (0, 2), (1, 1), (1, 3), (1, 2))
        ]
        own = pl.ds((yh * 4 + v) * ROW, ROW)
        return cps, here(src.at[own], dst.at[own])

    sr_cp, ch_cp = {}, {}

    def piece(q):
        p = q // 2
        own_cot[q].wait()
        arrived(fwd_cp[q])

        def step(i, carry):
            r = pl.ds(pl.multiple_of(i * 320, 320), 320)
            s[q, r, :] = (dot(ohg[p, r, :], cg[q]) * gc[p, r, 0:1]).astype(BF)
            return carry

        lax.fori_loop(0, 2, step, 0)
        sr_cp[q] = spread(p, s.at[q], sr.at[q])
        ch_cp[q] = remote(cg.at[q], ch.at[q], dc=1)

    piece(0)
    piece(2)
    a1_cp, a1_own = [], []
    for p in range(2):
        a1_cp.append([
            remote(w.at[yl, c, :, (vs[p] + d) % 4, :, half(p)], a1r.at[p, vs[p]], **way(p, dv=d))
            for d in (1, 3, 2)
        ])
        a1_own.append(here(w.at[yl, c, :, vs[p], :, half(p)], a1r.at[p, vs[p]]))
    pass_on(1)
    pass_on(3)
    for i in range(NP):
        pa_copy[i].wait()

        def act_step(j, carry):
            rows = pa[i % 2, pl.ds(j * 8, 8)].reshape(32, 2 * HID).astype(F32)
            gate, up = rows[:, :HID], rows[:, HID:]
            hid[pl.ds(pl.multiple_of(i * pt * 4 + j * 32, 32), 32), :] = (
                gate * jax.nn.sigmoid(gate) * up
            ).astype(BF)
            return carry

        lax.fori_loop(0, pt // 8, act_step, 0)
        if i + 2 < NP:
            pa_copy.append(here(pre.at[pl.ds((i + 2) * pt, pt)], pa.at[i % 2]))

    actx_cp, actx_own = [], []
    for p in range(2):

        def acts_step(i, carry):
            r = pl.ds(pl.multiple_of(i * 320, 320), 320)
            acts[p, r, :] = dot(ohx[p, r, :], hid[:, hh(p)]).astype(BF)
            return carry

        lax.fori_loop(0, 2, acts_step, 0)
    ahot[...] = dot(sel[...], hid[...]).astype(BF)
    eye = onehot(iota((TOK, TOK), 0) == iota((TOK, TOK), 1))
    aht[...] = dot(ahot[...], eye, TN).astype(BF).reshape(2, HID // 2, TOK)

    def ring_part(p, d, cc):
        return pl.ds(256 * ((c + cc) % 2) + 64 * ((us[p] + d) % 4), 64)

    for p in range(2):
        u = us[p]
        actx_cp.append([
            remote(acts.at[p, pl.ds(((u + d) % 4) * 160, 160)], actx.at[p, pl.ds(u * 160, 160)],
                   **way(p, du=d))
            for d in (1, 3, 2)
        ])
        actx_own.append(here(acts.at[p, pl.ds(u * 160, 160)], actx.at[p, pl.ds(u * 160, 160)]))
    at_cp, at_own = [], []
    for p in range(2):
        at_cp.append([])
        for cc in range(2):
            for d in range(4):
                src = aht.at[:, ring_part(p, d, cc), :]
                dst = at.at[p, :, :, pl.ds((cc * 4 + us[p]) * TOK, TOK)]
                if cc or d:
                    at_cp[p].append(remote(src, dst, **way(p, du=d, dc=cc)))
                else:
                    at_own.append(here(src, dst))

    o = iota((COLD, 128), 0)
    oj = sum((o >= ROW * k).astype(jnp.int32) for k in range(1, NJ))
    orem = o - ROW * oj
    ob = sum((orem >= CAP * k).astype(jnp.int32) for k in range(1, NX))
    want = ob * 160 + oj * CAP + (orem - CAP * ob)
    for k in range(COLD // 128):
        pm[:, pl.ds(k * 128, 128)] = onehot(want == iota((COLD, 128), 1) + k * 128)
    o = iota((4 * ROW, 4 * ROW), 0)
    oj = sum((o >= ROW * k).astype(jnp.int32) for k in range(1, 4))
    orem = o - ROW * oj
    ob = sum((orem >= CAP * k).astype(jnp.int32) for k in range(1, NX))
    px[...] = onehot(ob * ROW + oj * CAP + (orem - CAP * ob) == iota((4 * ROW, 4 * ROW), 1))

    def turn(src, dst):
        for k in range(2):
            r = pl.ds(k * 4 * ROW, 4 * ROW)
            dst[r, :] = dot(px[...], src[r, :]).astype(BF)

    yr_cp = {}

    def expert_hidden(n):
        q = ORDER[n]
        w_copy[q].wait()
        sr_cp[q][1].wait()
        arrived(sr_cp[q][0])
        rows = sr.at[q]
        if q >= 2:
            turn(sr.at[q], sp)
            rows = sp
        for h in range(2):
            for k in range(2):
                r = pl.ds(512 * h + 256 * k, 256)
                part = dot(rows[...], wq[q, h, k].reshape(256, DQ), NT)
                hacc[:, r] = part if n == 0 else hacc[:, r] + part

    def expert_weight(n):
        q = ORDER[n]
        rows = sp if q >= 2 else sr.at[q]
        for p in range(2):
            act = (actr.at[0], actb)[p]

            def wg_step(i, carry):
                r = pl.ds(pl.multiple_of(i * 256, 256), 256)
                wgs[pl.ds(pl.multiple_of(p * HALFHID + i * 256, 256), 256), :] = dot(
                    act[:, r], rows[...], TN
                ).astype(BF)
                return carry

            lax.fori_loop(0, 2, wg_step, 0)
        cr_cp = [
            remote(wgs.at[pl.ds(512 * h + 256 * ((c + 1) % 2), 256)], cr.at[n % 2, h], dc=1)
            for h in range(2)
        ]

        for cp in cr_cp:
            cp.wait()
        there, stay = (yl + 1) % 2, yl
        left(sr_cp[q][0])
        s[q, 0:256, :] = (
            wgs[pl.ds(512 * there + 256 * c, 256), :].astype(F32)
            + cr[n % 2, there].astype(F32)
        ).astype(BF)
        yr_cp[q] = remote(s.at[q, pl.ds(0, 256)], yr.at[q], dyl=1)
        wg[:, cols(q)] = (
            wgs[pl.ds(512 * stay + 256 * c, 256), :].astype(F32)
            + cr[n % 2, stay].astype(F32)
        ).astype(BF)

    a2_cp, a2_own, a3_cp, wh_cp, wh_own = [], [], [], [], []
    for p in range(2):
        a1_own[p].wait()
        arrived(a1_cp[p])
        for k in range(4):
            a2s[p, k] = sum(a1r[p, i, k].astype(F32) * hot_v[p][i] for i in range(4)).astype(BF)
        u = us[p]
        a2_cp.append([
            remote(a2s.at[p, (u + d) % 4], a2r.at[p, u], **way(p, du=d)) for d in (1, 3, 2)
        ])
        a2_own.append(here(a2s.at[p, u], a2r.at[p, u]))
    for p in range(2):
        a2_own[p].wait()
        arrived(a2_cp[p])
        a3s[p] = sum(a2r[p, k].astype(F32) * hot_u[p][k] for k in range(4)).astype(BF)
        a3_cp.append(remote(a3s.at[p], a3r.at[p], dyh=1))
    actr_cp, actr_own = [], []
    for p in range(2):
        actx_own[p].wait()
        arrived(actx_cp[p])

        def actp_step(i, carry):
            r = pl.ds(pl.multiple_of(i * 320, 320), 320)
            actp[p, r, :] = dot(pm[r, :], actx[p]).astype(BF)
            return carry

        lax.fori_loop(0, 2, actp_step, 0)
        a, b = spread(p, actp.at[p], actr.at[p])
        actr_cp.append(a)
        actr_own.append(b)

    mine = hot_y[0] * (yh == 0).astype(F32) + hot_y[1] * (yh == 1).astype(F32)
    for p in range(2):
        arrived([a3_cp[p]])
        ags[p] = (
            a3s[p].astype(F32) * mine + a3r[p].astype(F32) * (1.0 - mine)
        ).astype(BF)
        slot = wh.at[p, yl, vs[p]]
        wh_cp.append([
            remote(ags.at[p], slot, **way(p, dv=d, dyl=b))
            for b in range(2) for d in range(4) if b or d
        ])
        wh_own.append(here(ags.at[p], slot))

    piece(1)
    piece(3)
    sh = wgs
    diag = iota((TOK, TOK), 0) == iota((TOK, TOK), 1)
    hh_cp, hh_own, rs_cp, rs_own = [], [], [], []
    for p in range(2):
        at_own[p].wait()
        arrived(at_cp[p])
        wh_own[p].wait()
        arrived(wh_cp[p])
        for i in range(2):
            q = 2 * p + i
            arrived([ch_cp[q]])
            for b in range(2 * NX):
                m = mg[p, b]
                row = sum(
                    jnp.where(m[k:k + 1] == hotid, m[4 + k:5 + k], 0.0) for k in range(TOPK)
                )
                col = jnp.sum(jnp.where(diag, row, 0.0), axis=1, keepdims=True)
                block = (cg, ch)[b // NX][q, pl.ds((b % NX) * TOK, TOK), :]
                sh[pl.ds(b * TOK, TOK), :] = (block.astype(F32) * col).astype(BF)
            hp[q] = dot(at[p].reshape(128, 8 * TOK), sh[...]).astype(BF)
            part = dot(wh[p, :, :, :, pl.ds(i * DQ, DQ)].reshape(128, DQ), sh[...], NT)
            for k in range(8):
                t, r = pl.ds(k * 128, 128), pl.ds((k % 4) * 128, 128)
                if i == 0:
                    gc[k // 4, r, :] = part[:, k * 128:(k + 1) * 128]
                else:
                    hhs[p, :, :, t] = (
                        gc[k // 4, r, :] + part[:, k * 128:(k + 1) * 128]
                    ).astype(BF).reshape(2, 64, TOK)
        hh_cp.append([])
        for cc in range(2):
            for d in range(4):
                src = hhs.at[p, :, :, pl.ds((cc * 4 + (us[p] + d) % 4) * TOK, TOK)]
                dst = hht.at[p, :, pl.ds(256 * c + 64 * us[p], 64), :]
                if cc or d:
                    hh_cp[p].append(remote(src, dst, **way(p, du=d, dc=cc)))
                else:
                    hh_own.append(here(src, dst))
        rs_cp.append([])
        k = 1
        for a in range(2):
            for b in range(2):
                for d in range(4):
                    src = hp.at[
                        2 * p + (yh + a) % 2,
                        pl.ds(((yl + b) % 2) * 64 + ((vs[p] + d) % 4) * 16, 16),
                    ]
                    if a or b or d:
                        rs_cp[p].append(
                            remote(src, rsb.at[p, k], **way(p, dv=d, dyh=a, dyl=b))
                        )
                        k += 1
                    else:
                        rs_own.append(here(src, rsb.at[p, 0]))

    for p in range(2):
        actr_own[p].wait()
        arrived(actr_cp[p])
    turn(actr.at[1], actb)
    for n in range(2):
        expert_hidden(n)
        expert_weight(n)

    expert_hidden(2)
    expert_hidden(3)
    for p in range(2):
        left(actx_cp[p])
    hg = acts
    hgx_cp, hgx_own = [], []
    for p in range(2):
        if p == 0:
            hg[0] = hacc[:, hh(0)].astype(BF)
        else:
            for k in range(2):
                r = pl.ds(k * 4 * ROW, 4 * ROW)
                hg[1, r, :] = dot(px[...], hacc[r, hh(1)].astype(BF)).astype(BF)
        a, b = spread(p, hg.at[p], hgx.at[p])
        hgx_cp.append(a)
        hgx_own.append(b)

    g1_cp, g1_own, g2_cp, g2_own, g3_cp, g3_own = [], [], [], [], [], []
    for p in range(2):
        rs_own[p].wait()
        arrived(rs_cp[p])
        gp[p] = sum(rsb[p, k].astype(F32) for k in range(16)).astype(BF)
        g1_cp.append([remote(gp.at[p], g1.at[p, vs[p]], **way(p, dv=d)) for d in (1, 3, 2)])
        g1_own.append(here(gp.at[p], g1.at[p, vs[p]]))

    for p in range(2):
        g1_own[p].wait()
        arrived(g1_cp[p])
        g2_cp.append(remote(g1.at[p], g2.at[p, yh], dyh=1))
        g2_own.append(here(g1.at[p], g2.at[p, yh]))
    expert_weight(2)
    for p in range(2):
        g2_own[p].wait()
        arrived([g2_cp[p]])
        g3_cp.append([remote(g2.at[p], g3.at[p, us[p]], **way(p, du=d)) for d in (1, 3, 2)])
        g3_own.append(here(g2.at[p], g3.at[p, us[p]]))
    expert_weight(3)

    hgp = actp
    ret_cp, ret_own = [], []
    for p in range(2):
        left(actr_cp[p])
        hgx_own[p].wait()
        arrived(hgx_cp[p])
        for i in range(5):
            r = pl.ds(i * 128, 128)
            hgp[p, r, :] = dot(pm[:, r], hgx[p], TN).astype(BF)
        u = us[p]
        ret_cp.append([
            remote(hgp.at[p, pl.ds(((u + d) % 4) * 160, 160)], ret.at[p, pl.ds(u * 160, 160)],
                   **way(p, du=d))
            for d in (1, 3, 2)
        ])
        ret_own.append(here(hgp.at[p, pl.ds(u * 160, 160)], ret.at[p, pl.ds(u * 160, 160)]))

    for p in range(2):
        hh_own[p].wait()
        arrived(hh_cp[p])
    ahot[...] = (
        dot(eye, hht[0].reshape(HID, TOK), NT) + dot(eye, hht[1].reshape(HID, TOK), NT)
    ).astype(BF)

    for n, q in enumerate(ORDER):
        yr_cp[q].wait_recv()
        sent.append(yr_cp[q])
        wg[:, cols(q)] = (wg[:, cols(q)].astype(F32) + yr[q].astype(F32)).astype(BF)
    for p in range(2):
        ret_own[p].wait()
        arrived(ret_cp[p])
        for i in range(2):
            r, t = pl.ds(i * 256, 256), pl.ds(p * HALFHID + i * 256, 256)
            hid[:, t] = (dot(ohx[p], ret[p, :, r], TN) + dot(sel[...], ahot[:, t], TN)).astype(BF)

    own = (e1 == e).astype(F32)
    is_hot = jnp.sum(own * hotv, axis=0, keepdims=True)
    for p in range(2):
        g3_own[p].wait()
        arrived(g3_cp[p])
        for ut in range(4):
            for i in range(2):
                for vt in range(4):
                    r, k = pl.ds(64 * ut + 16 * vt, 16), cols(2 * p + i)
                    wg[r, k] = (
                        wg[r, k].astype(F32) * (1.0 - is_hot)
                        + g3[p, ut, i, vt].astype(F32) * is_hot
                    ).astype(BF)
    for cp in sent:
        cp.wait_send()


def vm(*shape, dtype=BF):
    return pltpu.VMEM(shape, dtype)


def run_main(cot, rt, gt, pre, w):
    anyw = pl.BlockSpec(memory_space=pl.ANY)
    vmem = pl.BlockSpec(memory_space=pltpu.VMEM)
    scratch = [
        vm(8, 128, dtype=F32),
        vm(NQ, SLOT, DQ), vm(NQ, SLOT, DQ), vm(2, 8, 8, 128, dtype=F32),
        vm(2, TOK // 4, TOPK, 2 * HID), vm(NQ, 2, 2, 4, 4, 16, DQ),
        vm(2, COLD, SLOT), vm(TOK, SLOT), vm(2, COLD, SLOT), vm(COLD, COLD),
        vm(4 * ROW, 4 * ROW), vm(2, COLD, 128, dtype=F32),
        vm(2, COLD, HALFHID), vm(2, COLD, HALFHID), vm(2, COLD, HALFHID), vm(2, COLD, HALFHID),
        vm(COLD, HALFHID),
        vm(NQ, COLD, DQ), vm(NQ, COLD, DQ), vm(COLD, DQ), vm(COLD, HID, dtype=F32),
        vm(2, COLD, HALFHID), vm(2, COLD, HALFHID),
        vm(HID, DQ), vm(2, 2, 256, DQ), vm(NQ, 256, DQ),
        vm(2, 4, 4, 16, HALF), vm(2, 4, 16, HALF), vm(2, 4, 16, HALF),
        vm(2, 16, HALF), vm(2, 16, HALF), vm(2, 16, HALF), vm(2, 2, 4, 16, HALF),
        vm(TOK, HID), vm(2, HID // 2, TOK), vm(2, 2, 64, 8 * TOK), vm(2, 2, HID // 2, TOK),
        vm(2, 2, 64, 8 * TOK), vm(NQ, 128, DQ),
        vm(2, 16, 16, DQ), vm(2, 16, DQ), vm(2, 4, 16, DQ), vm(2, 2, 4, 16, DQ),
        vm(2, 4, 2, 4, 16, DQ),
        pltpu.SemaphoreType.DMA((256,)), pltpu.SemaphoreType.DMA((256,)),
        pltpu.SemaphoreType.DMA((64,)),
    ]
    return pl.pallas_call(
        main_kernel,
        out_shape=(
            jax.ShapeDtypeStruct((SLOT, HID), BF),
            jax.ShapeDtypeStruct((256, D), BF),
        ),
        in_specs=[anyw, vmem, vmem, anyw, anyw],
        out_specs=(vmem, vmem),
        scratch_shapes=scratch,
        compiler_params=pltpu.CompilerParams(
            collective_id=0, has_side_effects=True, vmem_limit_bytes=61 * 1024 * 1024
        ),
        cost_estimate=pl.CostEstimate(
            flops=22 * 10**9, bytes_accessed=16 * 10**6, transcendentals=10**6
        ),
    )(cot, rt, gt, pre, w)


def grad_kernel(h, p, o):
    n = h.shape[0]
    back = h[...].astype(F32)
    rows = p[...].reshape(n, 2 * HID).astype(F32)
    gate, up = rows[:, :HID], rows[:, HID:]
    sig = jax.nn.sigmoid(gate)
    left = back * up * sig * (1.0 + gate * (1.0 - sig))
    right = back * gate * sig
    o[:, :, :HID] = left.astype(BF).reshape(n // TOPK, TOPK, HID)
    o[:, :, HID:] = right.astype(BF).reshape(n // TOPK, TOPK, HID)


def run_grad(hidden, pre):
    n = 32
    return pl.pallas_call(
        grad_kernel,
        grid=(TOK // n,),
        out_shape=jax.ShapeDtypeStruct((TOK, TOPK, 2 * HID), BF),
        in_specs=[
            pl.BlockSpec((n * TOPK, HID), lambda i: (i, 0)),
            pl.BlockSpec((n, TOPK, 2 * HID), lambda i: (i, 0, 0)),
        ],
        out_specs=pl.BlockSpec((n, TOPK, 2 * HID), lambda i: (i, 0, 0)),
        compiler_params=pltpu.CompilerParams(vmem_limit_bytes=24 * 1024 * 1024),
    )(hidden, pre)


def local(cotangent, routes, gates, pre_act, down_weight):
    hidden, weight = run_main(
        cotangent, routes.T, gates.T, pre_act, down_weight.reshape(2, 2, 4, 4, 16, D)
    )
    return run_grad(hidden, pre_act), weight[None]


def solution(mesh):
    in_specs = (
        P(("grp", "ep"), None),
        P(("grp", "ep"), None),
        P(("grp", "ep"), None),
        P(("grp", "ep"), None, None),
        P("ep", None, None),
    )
    out_specs = (P(("grp", "ep"), None, None), P("ep", "grp", None))
    return jax.shard_map(local, mesh=mesh, in_specs=in_specs, out_specs=out_specs, check_vma=False)
```
